32 devices in a mesh: dp: 4 (over z), expert: 4 (over y, core), tensor: 2 (over x).
Axes of the slice: x: 2, y: 2, z: 4, core: 2. Of those that a mesh axis runs over, the one named last changes fastest.
Arguments:
- tokens: bfloat16 [1024, 3072], P('expert', 'dp'), may hold values from -6 to 6
- route_ids: int32 [1024, 2], P('expert'), may hold values from 0 to 3, all different within a row; in each aligned block of 256 rows (0 to 255, 256 to 511, ...) at most 128 rows name the same one
- gates: float32 [1024, 2], P('expert'), may hold values from 0.2 to 1
- w_gate: bfloat16 [4, 3072, 8192], P('expert', 'dp', 'tensor'), may hold values from -0.109375 to 0.109375
- w_up: bfloat16 [4, 3072, 8192], P('expert', 'dp', 'tensor'), may hold values from -0.109375 to 0.109375
- w_down: bfloat16 [4, 8192, 3072], P('expert', 'tensor', 'dp'), may hold values from -0.0625 to 0.0625
Outputs:
- mixed: bfloat16 [1024, 3072], P('expert', 'dp')
The draws below stay inside these ranges and needn't reach their ends.
Inputs may be any that keep to these rules, and one draw needn't show every extreme that they name: `route_ids`: each token names two different experts. Among the 256 tokens of one index of expert, no expert is named by more than 128 tokens, a bound that some block reaches.
All inputs are finite; a program needn't handle non-finite values.
Results may differ from the reference program's by a relative error of at most 0.025.
Values may be sent and summed in bfloat16 or wider, within the bound.
No kernel may reach another device: no remote copies, remote signals or barrier semaphores. Data moves between devices by JAX's collectives and lax.ppermute only.
A program may use at most 64 MiB of HBM per device.

```python
import math
import jax
import jax.numpy as jnp
import numpy as np
from jax import lax

D = 3072
FF = 8192
TOK_E = 256
EXPERTS = 4
TOKENS = 1024
CAP = 128
WIDTH_BLOCKS = 4


def level_of(key, shape, cuts, low, high):
    def one(axis_at, shards_of):
        heights = jax.random.uniform(jax.random.fold_in(jax.random.fold_in(key, 6), axis_at), (shards_of,), jnp.float32, low / len(cuts), high / len(cuts))
        return jnp.repeat(jnp.exp(heights), shape[axis_at] // shards_of).reshape((-1,) + (1,) * (len(shape) - axis_at - 1))

    gain = one(*cuts[0])
    for cut in cuts[1:]:
        gain = gain * one(*cut)
    return gain


def deal_out(stream_key, own, number, rows, amount, top, limit, lean):
    sequence = jax.random.permutation(stream_key, amount)
    crowded, common = load_shares(amount, rows * top, limit, lean, True), load_shares(amount, rows * top, limit, lean, False)
    places = jnp.arange(amount)

    def named(sizes, turn):
        used = int((sizes > 0).sum())
        fixed = max(1, used // 4)
        passed = fixed + (places - fixed + turn * (used - fixed)) % max(1, amount - fixed)
        return jnp.zeros((amount,), jnp.int32).at[sequence[jnp.where(places < fixed, places, passed)]].set(jnp.asarray(sizes, jnp.int32))

    sizes = jnp.where(number % 4 == 0, named(crowded, number // 4), named(common, number - number // 4 - 1))
    mixed = jax.random.permutation(jax.random.fold_in(own, 3), amount)
    source_of, receiver = mixed[0:amount // 2 * 2:2], mixed[1:amount // 2 * 2:2]
    margin = jnp.minimum(sizes[source_of] - 1, limit - sizes[receiver]) // 2
    margin = jnp.where((source_of == sequence[0]) | (receiver == sequence[0]) | (sizes[receiver] == 0), 0, jnp.maximum(margin, 0))
    passed = jax.random.randint(jax.random.fold_in(own, 4), (amount // 2,), 0, 1 << 20) % (margin + 1)
    sizes = sizes.at[source_of].add(-passed).at[receiver].add(passed)
    labels = jnp.searchsorted(jnp.cumsum(sizes), jnp.arange(rows * top), side="right").astype(jnp.int32)
    table = labels.reshape(top, rows).T
    table = table[jax.random.permutation(jax.random.fold_in(own, 1), rows)]
    turn = jax.random.randint(jax.random.fold_in(own, 2), (rows, 1), 0, top)
    return jnp.take_along_axis(table, (jnp.arange(top)[None, :] + turn) % top, axis=1)


def load_shares(amount, total, most, lean, full):
    weights = [(1 << 20) // math.isqrt(standing ** lean) + 1 for standing in range(1, amount + 1)]
    largest = most if full else min(most, max(-(-total // amount), total * weights[0] // sum(weights)))
    least = 1 if total - largest >= amount - 1 else 0
    counts, spare = [largest] + [least] * (amount - 1), total - largest - least * (amount - 1)
    while spare > 0:
        movable = [i for i in range(1, amount) if counts[i] < largest] or [i for i in range(1, amount) if counts[i] < most]
        pool, remaining = sum([weights[i] for i in movable]), spare
        for i in movable:
            addition = min(most - counts[i], max(1, remaining * weights[i] // pool), spare)
            counts[i] = counts[i] + addition
            spare = spare - addition
    return np.array(counts)


def bell_draw(key, dims, width, reach, cuts=(), kind=jnp.bfloat16):
    values = width * jax.random.normal(key, dims, jnp.float32)
    if cuts:
        values = values * level_of(key, dims, cuts, -0.22, 0.18)
    return jnp.clip(values, -reach, reach).astype(kind)


def setup_inputs(seed: int = 0) -> dict:
    key_list = jax.random.split(jax.random.key(seed), 7)
    tokens = bell_draw(key_list[0], (TOKENS, D), 1.0, 6.0, ((0, 4), (1, 4)))
    route_ids_keys = jax.random.split(jax.random.fold_in(key_list[1], 1), TOKENS // TOK_E)
    route_ids_turns = jax.random.permutation(jax.random.fold_in(key_list[1], 3), TOKENS // TOK_E)
    route_ids = jax.vmap(lambda own, number: deal_out(jax.random.fold_in(key_list[1], 2), own, number, TOK_E, EXPERTS, 2, CAP, 2))(route_ids_keys, route_ids_turns).reshape((TOKENS, 2))
    gates = jnp.clip(0.2 + 0.8 * jax.random.uniform(key_list[2], (TOKENS, 2), jnp.float32) ** level_of(key_list[2], (TOKENS, 2), ((0, 4),), -0.2, 0.2), 0.2, 1.0)
    w_gate = bell_draw(key_list[3], (EXPERTS, D, FF), D ** -0.5, 0.109375, ((0, 4), (1, 4), (2, 2)))
    w_up = bell_draw(key_list[4], (EXPERTS, D, FF), D ** -0.5, 0.109375, ((0, 4), (1, 4), (2, 2)))
    w_down = bell_draw(key_list[5], (EXPERTS, FF, D), FF ** -0.5, 0.0625, ((0, 4), (1, 2), (2, 4)))
    return dict(tokens=tokens, route_ids=route_ids, gates=gates, w_gate=w_gate, w_up=w_up, w_down=w_down)


def slot_index(route_group):
    flat = route_group.reshape(-1)
    hits = (flat[:, None] == jnp.arange(EXPERTS, dtype=jnp.int32)[None, :]).astype(jnp.int32)
    before = jnp.cumsum(hits, axis=0) - hits
    rank = jnp.sum(before * hits, axis=1)
    return (rank * EXPERTS + flat).reshape(-1, 2).astype(jnp.int32)


def reference(tokens, route_ids, gates, w_gate, w_up, w_down):
    groups = tokens.reshape(EXPERTS, TOK_E, D)
    where = jax.vmap(slot_index)(route_ids.reshape(EXPERTS, TOK_E, 2))

    def fill(rows, place):
        buffer = jnp.zeros((CAP * EXPERTS, D), jnp.bfloat16)
        return buffer.at[place.reshape(-1)].set(jnp.repeat(rows, 2, axis=0))

    sent = jax.vmap(fill)(groups, where).reshape(EXPERTS, CAP, EXPERTS, D)
    block_width = D // WIDTH_BLOCKS

    def run_expert(number):
        rows = sent[:, :, number, :].transpose(1, 0, 2).reshape(CAP * EXPERTS, D).astype(jnp.float32)
        wg = w_gate[number].astype(jnp.float32)
        wu = w_up[number].astype(jnp.float32)
        gate = jnp.zeros((CAP * EXPERTS, FF), jnp.float32)
        up_sum = jnp.zeros((CAP * EXPERTS, FF), jnp.float32)
        for block in range(WIDTH_BLOCKS):
            lower = block * block_width
            part = rows[:, lower:lower + block_width]
            g_part = jnp.dot(part, wg[lower:lower + block_width], preferred_element_type=jnp.float32)
            u_part = jnp.dot(part, wu[lower:lower + block_width], preferred_element_type=jnp.float32)
            g_part, u_part = lax.optimization_barrier((g_part.astype(jnp.bfloat16), u_part.astype(jnp.bfloat16)))
            gate = gate + g_part.astype(jnp.float32)
            up_sum = up_sum + u_part.astype(jnp.float32)
        hidden = (jax.nn.silu(gate) * up_sum).astype(jnp.bfloat16)
        result = jnp.dot(hidden.astype(jnp.float32), w_down[number].astype(jnp.float32), preferred_element_type=jnp.float32)
        return result.astype(jnp.bfloat16).reshape(CAP, EXPERTS, D)

    done = lax.map(run_expert, jnp.arange(EXPERTS, dtype=jnp.int32))
    table = done.transpose(2, 1, 0, 3).reshape(EXPERTS, CAP * EXPERTS, D)

    def combine(rows_table, place, weights):
        first = rows_table[place[:, 0]].astype(jnp.float32)
        second = rows_table[place[:, 1]].astype(jnp.float32)
        return (weights[:, 0:1] * first + weights[:, 1:2] * second).astype(jnp.bfloat16)

    mixed = jax.vmap(combine)(table, where, gates.reshape(EXPERTS, TOK_E, 2))
    return mixed.reshape(TOKENS, D)
```

```python
import jax
import jax.numpy as jnp
import numpy as np
from jax import lax
from jax.sharding import PartitionSpec as P

F32, BF16 = jnp.float32, jnp.bfloat16
CHUNK = 32


def places_of(ids, experts):
    hits = ids[:, :, None] == jnp.arange(experts, dtype=jnp.int32)
    named = jnp.sum(hits.astype(F32), axis=1).astype(BF16)
    n = ids.shape[0]
    earlier = (jnp.arange(n)[:, None] > jnp.arange(n)[None, :]).astype(BF16)
    before = jnp.dot(earlier, named, preferred_element_type=F32)
    rank = jnp.sum(jnp.where(hits, before[:, None, :], 0.0), axis=2).astype(jnp.int32)
    again = (ids[:, 0] == ids[:, 1]).astype(jnp.int32)
    rank = rank + jnp.stack([jnp.zeros_like(again), again], axis=1)
    return rank * experts + ids


def chunk_order(experts, per):
    head = max(1, per // 2)
    order = [(0, i) for i in range(head)]
    order += [(j, i) for j in range(1, experts) for i in range(per)]
    return order + [(0, i) for i in range(head, per)]


def pick(options, index):
    out = options[-1]
    for k in range(len(options) - 2, -1, -1):
        out = jnp.where(index == k, options[k], out)
    return out


def local(tokens, route_ids, gates, w_gate, w_up, w_down):
    experts = lax.axis_size("expert")
    depth = lax.axis_size("dp")
    tensors = lax.axis_size("tensor")
    z = lax.axis_index("dp")
    e = lax.axis_index("expert")
    n, width = tokens.shape
    units = w_gate.shape[2]
    capacity = max(3 * n // 8, 2 * n // experts)
    capacity = (capacity + 15) // 16 * 16
    half = capacity // 2
    m = CHUNK if half % CHUNK == 0 else 16
    per = half // m
    order = chunk_order(experts, per)
    chunks = len(order)
    last = depth - 1

    places = places_of(route_ids, experts)
    rows = []
    for j in range(experts):
        lines = jnp.arange(capacity, dtype=jnp.int32) * experts + (e ^ j)
        chosen = (lines[:, None] == places[None, :, 0]) | (lines[:, None] == places[None, :, 1])
        picked = jnp.dot(chosen.astype(BF16), tokens, preferred_element_type=F32).astype(BF16)
        if j:
            picked = lax.ppermute(picked, "expert", [(a, a ^ j) for a in range(experts)])
        rows.append(picked)

    nothing = jnp.zeros((m, width), BF16)

    def chunk_rows(index, way):
        if not 0 <= index < chunks:
            return nothing
        j, i = order[index]
        return lax.slice_in_dim(rows[j], way * half + i * m, way * half + (i + 1) * m)

    up = [(a, a + 1) for a in range(last)]
    down = [(a + 1, a) for a in range(last)]
    wg, wu, wd = w_gate[0], w_up[0], w_down[0]
    ticks = chunks + 2 * last
    got = [None, None]
    got_hidden = [None, None]
    table = []
    names = np.full((depth, (ticks - last) * 2 * m, 2), -1, np.int32)
    for s in range(ticks):
        total = [None, None]
        if s < chunks + last:
            block = jnp.concatenate(
                [
                    pick([chunk_rows(s - a, 0) for a in range(depth)], z),
                    pick([chunk_rows(s - last + a, 1) for a in range(depth)], z),
                ]
            )
            g = jnp.dot(block, wg, preferred_element_type=F32).astype(BF16)
            u = jnp.dot(block, wu, preferred_element_type=F32).astype(BF16)
            g, u = lax.optimization_barrier((g, u))
            for way in range(2):
                part = [g[way * m : (way + 1) * m].astype(F32), u[way * m : (way + 1) * m].astype(F32)]
                if s:
                    part = [a + b.astype(F32) for a, b in zip(part, got[way])]
                total[way] = part
                if s < chunks + last - 1:
                    got[way] = [lax.ppermute(a.astype(BF16), "dp", up if way == 0 else down) for a in part]
        if s < last:
            continue
        hidden = []
        for way in range(2):
            owner = last if way == 0 else 0
            if total[way] is not None:
                h = (jax.nn.silu(total[way][0]) * total[way][1]).astype(BF16)
                if s > last:
                    h = jnp.where(z == owner, h, got_hidden[way])
            else:
                h = got_hidden[way]
            if s < ticks - 1:
                got_hidden[way] = lax.ppermute(h, "dp", down if way == 0 else up)
            hidden.append(h)
        out = jnp.dot(jnp.concatenate(hidden), wd, preferred_element_type=F32).astype(BF16)
        if tensors == 2:
            other = lax.ppermute(out, "tensor", [(0, 1), (1, 0)])
            out = (out.astype(F32) + other.astype(F32)).astype(BF16)
        else:
            out = lax.psum(out, "tensor")
        for way in range(2):
            piece = out[way * m : (way + 1) * m]
            pairs = []
            moved = False
            for a in range(depth):
                index = s - last - (last - a if way == 0 else a)
                if not 0 <= index < chunks:
                    continue
                j, i = order[index]
                moved = moved or j > 0
                pairs += [(a * experts + b, a * experts + (b ^ j)) for b in range(experts)]
                at = ((s - last) * 2 + way) * m
                names[a, at : at + m, 0] = way * half + i * m + np.arange(m)
                names[a, at : at + m, 1] = j
            if moved:
                piece = lax.ppermute(piece, ("dp", "expert"), pairs)
            table.append(piece)
    mine = lax.dynamic_index_in_dim(jnp.asarray(names), z, 0, keepdims=False)
    label = jnp.where(mine[:, 0] < 0, -1, mine[:, 0] * experts + (e ^ mine[:, 1]))
    filled = jnp.concatenate(table)
    mixed = jnp.zeros((n, width), F32)
    for k in range(2):
        chosen = (places[:, k : k + 1] == label[None, :]).astype(BF16)
        mixed += gates[:, k : k + 1] * jnp.dot(chosen, filled, preferred_element_type=F32)
    return mixed.astype(BF16)


def solution(mesh):
    return jax.shard_map(
        local,
        mesh=mesh,
        in_specs=(
            P("expert", "dp"),
            P("expert", None),
            P("expert", None),
            P("expert", "dp", "tensor"),
            P("expert", "dp", "tensor"),
            P("expert", "tensor", "dp"),
        ),
        out_specs=P("expert", "dp"),
        check_vma=False,
    )
```

```python
import jax
import jax.numpy as jnp
from jax import lax
from jax.sharding import PartitionSpec as P

F32, BF16 = jnp.float32, jnp.bfloat16
CHUNK = 32


def places_of(ids, experts):
    hits = ids[:, :, None] == jnp.arange(experts, dtype=jnp.int32)
    named = jnp.sum(hits.astype(F32), axis=1).astype(BF16)
    n = ids.shape[0]
    earlier = (jnp.arange(n)[:, None] > jnp.arange(n)[None, :]).astype(BF16)
    before = jnp.dot(earlier, named, preferred_element_type=F32)
    rank = jnp.sum(jnp.where(hits, before[:, None, :], 0.0), axis=2).astype(jnp.int32)
    again = (ids[:, 0] == ids[:, 1]).astype(jnp.int32)
    rank = rank + jnp.stack([jnp.zeros_like(again), again], axis=1)
    return rank * experts + ids


def chunk_order(experts, per):
    head = max(1, per // 2)
    order = [(0, i) for i in range(head)]
    order += [(j, i) for j in range(1, experts) for i in range(per)]
    return order + [(0, i) for i in range(head, per)]


def pick(options, index):
    out = options[-1]
    for k in range(len(options) - 2, -1, -1):
        out = jnp.where(index == k, options[k], out)
    return out


def local(tokens, route_ids, gates, w_gate, w_up, w_down):
    experts = lax.axis_size("expert")
    depth = lax.axis_size("dp")
    tensors = lax.axis_size("tensor")
    z = lax.axis_index("dp")
    e = lax.axis_index("expert")
    n, width = tokens.shape
    units = w_gate.shape[2]
    capacity = max(3 * n // 8, 2 * n // experts)
    capacity = (capacity + 15) // 16 * 16
    half = capacity // 2
    m = CHUNK if half % CHUNK == 0 else 16
    per = half // m
    order = chunk_order(experts, per)
    chunks = len(order)
    last = depth - 1

    even = e % 2 == 0
    spot = [jnp.where(even, z, last - z), jnp.where(even, last - z, z)]
    climb = [(a * experts + b, (a + 1) * experts + b) for a in range(last) for b in range(experts)]
    flows = [
        [(a, c) if a % experts % 2 == f else (c, a) for a, c in climb] for f in range(2)
    ]

    places = places_of(route_ids, experts)
    rows = []
    for j in range(experts):
        lines = jnp.arange(capacity, dtype=jnp.int32) * experts + (e ^ j)
        chosen = (lines[:, None] == places[None, :, 0]) | (lines[:, None] == places[None, :, 1])
        picked = jnp.dot(chosen.astype(BF16), tokens, preferred_element_type=F32).astype(BF16)
        if j:
            picked = lax.ppermute(picked, "expert", [(a, a ^ j) for a in range(experts)])
        rows.append(picked)

    nothing = jnp.zeros((m, width), BF16)

    def chunk_rows(index, f):
        if not 0 <= index < chunks:
            return nothing
        j, i = order[index]
        return lax.slice_in_dim(rows[j], f * half + i * m, f * half + (i + 1) * m)

    wg, wu, wd = w_gate[0], w_up[0], w_down[0]
    sums_end = chunks + last
    got = [None, None]
    act = [None, None]
    held = [{}, {}]
    outs = []
    for s in range(chunks + 2 * last + 1):
        if s < sums_end:
            block = [pick([chunk_rows(s - a, f) for a in range(depth)], spot[f]) for f in range(2)]
            if s > 1:
                block = [jnp.where(jnp.isnan(sent[:m, :1]), nothing, b) for b in block]
            block = jnp.concatenate(block)
            g = jnp.dot(block, wg, preferred_element_type=F32).astype(BF16)
            u = jnp.dot(block, wu, preferred_element_type=F32).astype(BF16)
            g, u = lax.optimization_barrier((g, u))
        for f in range(2):
            send = []
            came = got[f]
            if s < sums_end:
                part = jnp.concatenate([g[f * m : (f + 1) * m], u[f * m : (f + 1) * m]]).astype(F32)
                if s:
                    part = part + came[: 2 * m].astype(F32)
                if s < sums_end - 1:
                    send.append(part.astype(BF16))
                if s >= last:
                    fresh = (jax.nn.silu(part[:m]) * part[m:]).astype(BF16)
                else:
                    fresh = None
            o = 1 - f
            first = last + 1 if f == 0 else last
            if first <= s < first + chunks + last:
                h = act[o]
                if s > first:
                    arrived = came[-m:]
                    h = arrived if h is None else jnp.where(spot[f] == 0, h, arrived)
                held[o][s - first] = h
                if s < first + chunks + last - 1:
                    send.append(h)
            act[f] = fresh if s < sums_end else None
            if send:
                message = send[0] if len(send) == 1 else jnp.concatenate(send)
                got[f] = lax.ppermute(message, ("dp", "expert"), flows[f])
                sent = message if f == 0 else sent
            if f == 0 and s - first in held[0]:
                q = s - first
                both = jnp.concatenate([held[0][q], held[1][q]])
                outs.append(jnp.dot(both, wd, preferred_element_type=F32).astype(BF16))

    def across(part):
        if tensors == 2:
            other = lax.ppermute(part, "tensor", [(0, 1), (1, 0)])
            return (part.astype(F32) + other.astype(F32)).astype(BF16)
        return lax.psum(part, "tensor")

    def finished(start, stop):
        return [
            jnp.concatenate(
                [
                    pick([outs[c + a][f * m : (f + 1) * m] for a in range(depth)], spot[1 - f])
                    for c in range(start, stop)
                ]
            )
            for f in range(2)
        ]

    yields = [jnp.zeros((n, width), F32), jnp.zeros((n, width), F32)]
    spans = []
    for index, (j, i) in enumerate(order):
        if spans and spans[-1][0] == j:
            spans[-1][2] = index + 1
        else:
            spans.append([j, index, index + 1, i])
    for j, start, stop, i in spans:
        size = (stop - start) * m
        part = across(jnp.concatenate(finished(start, stop)))
        if j:
            part = lax.ppermute(part, "expert", [(a, a ^ j) for a in range(experts)])
        ranks = jnp.arange(size, dtype=jnp.int32) + i * m
        ranks = jnp.concatenate([ranks, ranks + half])
        label = ranks * experts + (e ^ j)
        for k in range(2):
            chosen = (places[:, k : k + 1] == label[None, :]).astype(BF16)
            yields[k] += jnp.dot(chosen, part, preferred_element_type=F32)
    mixed = gates[:, 0:1] * yields[0] + gates[:, 1:2] * yields[1]
    return mixed.astype(BF16)


def solution(mesh):
    return jax.shard_map(
        local,
        mesh=mesh,
        in_specs=(
            P("expert", "dp"),
            P("expert", None),
            P("expert", None),
            P("expert", "dp", "tensor"),
            P("expert", "dp", "tensor"),
            P("expert", "tensor", "dp"),
        ),
        out_specs=P("expert", "dp"),
        check_vma=False,
    )
```

```python
import jax
import jax.numpy as jnp
from jax import lax
from jax.sharding import PartitionSpec as P

F32, BF16 = jnp.float32, jnp.bfloat16


def places_of(ids, experts):
    hits = ids[:, :, None] == jnp.arange(experts, dtype=jnp.int32)
    named = jnp.sum(hits.astype(F32), axis=1).astype(BF16)
    n = ids.shape[0]
    earlier = (jnp.arange(n)[:, None] > jnp.arange(n)[None, :]).astype(BF16)
    before = jnp.dot(earlier, named, preferred_element_type=F32)
    rank = jnp.sum(jnp.where(hits, before[:, None, :], 0.0), axis=2).astype(jnp.int32)
    again = (ids[:, 0] == ids[:, 1]).astype(jnp.int32)
    rank = rank + jnp.stack([jnp.zeros_like(again), again], axis=1)
    return rank * experts + ids


def local(tokens, route_ids, gates, w_gate, w_up, w_down):
    experts = lax.axis_size("expert")
    tensors = lax.axis_size("tensor")
    e = lax.axis_index("expert")
    n, width = tokens.shape
    units = w_gate.shape[2]
    capacity = max(3 * n // 8, 2 * n // experts)
    capacity = (capacity + 15) // 16 * 16
    places = places_of(route_ids, experts)
    rows = []
    for j in range(experts):
        lines = jnp.arange(capacity, dtype=jnp.int32) * experts + (e ^ j)
        chosen = (lines[:, None] == places[None, :, 0]) | (lines[:, None] == places[None, :, 1])
        picked = jnp.dot(chosen.astype(BF16), tokens, preferred_element_type=F32).astype(BF16)
        if j:
            picked = lax.ppermute(picked, "expert", [(a, a ^ j) for a in range(experts)])
        rows.append(picked)

    wg, wu, wd = w_gate[0], w_up[0], w_down[0]
    yields = [jnp.zeros((n, width), F32), jnp.zeros((n, width), F32)]
    for j in range(experts):
        g = jnp.dot(rows[j], wg, preferred_element_type=F32).astype(BF16)
        u = jnp.dot(rows[j], wu, preferred_element_type=F32).astype(BF16)
        both = jnp.concatenate([g, u], axis=1)
        both = lax.psum_scatter(both, "dp", scatter_dimension=0, tiled=True).astype(F32)
        h = (jax.nn.silu(both[:, :units]) * both[:, units:]).astype(BF16)
        h = lax.all_gather(h, "dp", axis=0, tiled=True)
        part = jnp.dot(h, wd, preferred_element_type=F32).astype(BF16)
        if tensors == 2:
            other = lax.ppermute(part, "tensor", [(0, 1), (1, 0)])
            part = (part.astype(F32) + other.astype(F32)).astype(BF16)
        else:
            part = lax.psum(part, "tensor")
        if j:
            part = lax.ppermute(part, "expert", [(a, a ^ j) for a in range(experts)])
        label = jnp.arange(capacity, dtype=jnp.int32) * experts + (e ^ j)
        for k in range(2):
            chosen = (places[:, k : k + 1] == label[None, :]).astype(BF16)
            yields[k] += jnp.dot(chosen, part, preferred_element_type=F32)
    mixed = gates[:, 0:1] * yields[0] + gates[:, 1:2] * yields[1]
    return mixed.astype(BF16)


def solution(mesh):
    return jax.shard_map(
        local,
        mesh=mesh,
        in_specs=(
            P("expert", "dp"),
            P("expert", None),
            P("expert", None),
            P("expert", "dp", "tensor"),
            P("expert", "dp", "tensor"),
            P("expert", "tensor", "dp"),
        ),
        out_specs=P("expert", "dp"),
        check_vma=False,
    )
```

```python
import jax
import jax.numpy as jnp
from jax import lax
from jax.experimental import pallas as pl
from jax.experimental.pallas import tpu as pltpu
from jax.sharding import PartitionSpec as P

F32, BF16 = jnp.float32, jnp.bfloat16
CHUNK = 32


def places_of(ids, experts):
    n = ids.shape[1]
    hits = ids[:, None, :] == jnp.arange(experts, dtype=jnp.int32)[None, :, None]
    named = (hits[0] | hits[1]).astype(BF16)
    earlier = (jnp.arange(n)[:, None] < jnp.arange(n)[None, :]).astype(BF16)
    before = jnp.dot(named, earlier, preferred_element_type=F32)
    rank = jnp.sum(jnp.where(hits, before[None], 0.0), axis=1).astype(jnp.int32)
    return rank * experts + ids


def chunk_order(experts, per):
    head = max(1, per // 2)
    order = [(0, i) for i in range(head)]
    order += [(j, i) for j in range(1, experts) for i in range(per)]
    return order + [(0, i) for i in range(head, per)]


def pick(options, index):
    out = options[-1]
    for k in range(len(options) - 2, -1, -1):
        out = jnp.where(index == k, options[k], out)
    return out


WHOLE = pl.BlockSpec(memory_space=pltpu.VMEM)
SCALAR = pl.BlockSpec(memory_space=pltpu.SMEM)
LIGHT = pl.CostEstimate(flops=0, bytes_accessed=0, transcendentals=0)


def call(body, name, shapes, *args):
    specs = [SCALAR if a.dtype == jnp.int32 else WHOLE for a in args]
    return pl.pallas_call(
        body,
        name=name,
        out_shape=shapes,
        in_specs=specs,
        out_specs=[WHOLE] * len(shapes),
        cost_estimate=LIGHT,
        compiler_params=pltpu.CompilerParams(vmem_limit_bytes=16 * 2**20),
    )(*args)


def width_of(columns):
    return 512 if columns % 512 == 0 else columns


def over_columns(columns, step):
    wide = width_of(columns)

    def body(i, carry):
        step(pl.ds(pl.multiple_of(i * wide, wide), wide))
        return carry

    lax.fori_loop(0, columns // wide, body, 0)


def combine(m, units, f, first, came, partial, act, summing, sending, fresh, owner):
    args, use = [], {}

    def take(key, value):
        if value is not None:
            use[key] = len(args)
            args.append(value)

    take("owner", owner if act is not None and came is not None else None)
    take("came", came)
    if summing:
        take("g", partial[0])
        take("u", partial[1])
    take("act", act)
    sums = 2 * m if summing and sending else 0
    hidden = act is not None or (came is not None and came.shape[0] % (2 * m) == m)
    rows = sums + (m if hidden else 0)
    shapes = []
    if rows:
        shapes.append(jax.ShapeDtypeStruct((rows, units), BF16))
    if fresh:
        shapes.append(jax.ShapeDtypeStruct((m, units), BF16))

    def body(*refs):
        ins, outs = refs[: len(args)], refs[len(args) :]
        message = outs[0] if rows else None

        def get(key):
            return ins[use[key]] if key in use else None

        came_ref, act_ref = get("came"), get("act")

        def step(cols):
            if summing:
                total = []
                for k, key in enumerate(("g", "u")):
                    value = get(key)[f * m : (f + 1) * m, cols].astype(F32)
                    if not first:
                        value = value + came_ref[k * m : (k + 1) * m, cols].astype(F32)
                    total.append(value)
                    if sending:
                        message[k * m : (k + 1) * m, cols] = value.astype(BF16)
                if fresh:
                    outs[-1][:, cols] = (total[0] / (1.0 + jnp.exp(-total[0])) * total[1]).astype(BF16)
            if hidden:
                if act_ref is None:
                    h = came_ref[came.shape[0] - m :, cols]
                elif "owner" in use:
                    h = jnp.where(get("owner")[0] != 0, act_ref[:, cols], came_ref[came.shape[0] - m :, cols])
                else:
                    h = act_ref[:, cols]
                message[sums:, cols] = h

        over_columns(units, step)

    return call(body, "combine", shapes, *args)


def project(block, wg, wu, tie):
    def body(*refs):
        x_ref, g_w, u_w = refs[:3]
        g_ref, u_ref = refs[-2:]

        def step(cols):
            x = x_ref[...]
            g_ref[:, cols] = jnp.dot(x, g_w[:, cols], preferred_element_type=F32).astype(BF16)
            u_ref[:, cols] = jnp.dot(x, u_w[:, cols], preferred_element_type=F32).astype(BF16)

        over_columns(wg.shape[1], step)

    shape = jax.ShapeDtypeStruct((block.shape[0], wg.shape[1]), BF16)
    return call(body, "project", [shape, shape], block, wg, wu, *tie)


def lower(m, one, two, wd):
    def body(one_ref, two_ref, w_ref, out_ref):
        def step(cols):
            h = jnp.concatenate([r[r.shape[0] - m :, :] for r in (one_ref, two_ref)])
            out_ref[:, cols] = jnp.dot(h, w_ref[:, cols], preferred_element_type=F32).astype(BF16)

        columns = wd.shape[1]
        wide = 256 if columns % 256 == 0 else columns

        def loop(i, carry):
            step(pl.ds(pl.multiple_of(i * wide, wide), wide))
            return carry

        lax.fori_loop(0, columns // wide, loop, 0)

    shape = jax.ShapeDtypeStruct((2 * m, wd.shape[1]), BF16)
    return call(body, "lower", [shape], one, two, wd)[0]


def local(tokens, route_ids, gates, w_gate, w_up, w_down):
    experts = lax.axis_size("expert")
    depth = lax.axis_size("dp")
    tensors = lax.axis_size("tensor")
    z = lax.axis_index("dp")
    e = lax.axis_index("expert")
    n, width = tokens.shape
    units = w_gate.shape[2]
    capacity = max(3 * n // 8, 2 * n // experts)
    capacity = (capacity + 15) // 16 * 16
    half = capacity // 2
    m = CHUNK if half % CHUNK == 0 else 16
    per = half // m
    order = chunk_order(experts, per)
    chunks = len(order)
    last = depth - 1

    even = e % 2 == 0
    spot = [jnp.where(even, z, last - z), jnp.where(even, last - z, z)]
    climb = [(a * experts + b, (a + 1) * experts + b) for a in range(last) for b in range(experts)]
    flows = [
        [(a, c) if a % experts % 2 == f else (c, a) for a, c in climb] for f in range(2)
    ]

    places = places_of(route_ids.T, experts)

    def rows_for(j, tie=None):
        lines = jnp.arange(capacity, dtype=jnp.int32) * experts + (e ^ j)
        chosen = (lines[:, None] == places[0][None, :]) | (lines[:, None] == places[1][None, :])
        if tie is not None:
            chosen = chosen & ~jnp.isnan(tie)
        picked = jnp.dot(chosen.astype(BF16), tokens, preferred_element_type=F32).astype(BF16)
        if j:
            picked = lax.ppermute(picked, "expert", [(a, a ^ j) for a in range(experts)])
        return picked

    rows = [rows_for(0)] + [None] * (experts - 1)
    nothing = jnp.zeros((m, width), BF16)

    def chunk_rows(index, f):
        if not 0 <= index < chunks:
            return nothing
        j, i = order[index]
        return lax.slice_in_dim(rows[j], f * half + i * m, f * half + (i + 1) * m)

    wg, wu, wd = w_gate[0], w_up[0], w_down[0]
    sums_end = chunks + last
    owners = [(spot[f] == 0).astype(jnp.int32).reshape(1) for f in range(2)]
    got = [None, None]
    act = [None, None]
    held = [{}, {}]
    outs = []
    partial = None

    def round_rows(s):
        return jnp.concatenate(
            [pick([chunk_rows(s - a, f) for a in range(depth)], spot[f]) for f in range(2)]
        )

    partial = project(round_rows(0), wg, wu, ())
    for s in range(chunks + 2 * last + 1):
        summing = s < sums_end
        for f in range(2):
            o = 1 - f
            first = last + 1 if f == 0 else last
            carries = first <= s < first + chunks + last
            came = got[f] if s else None
            if not (summing or carries):
                continue
            result = combine(
                m,
                units,
                f,
                s == 0,
                came,
                partial,
                act[o] if carries else None,
                summing,
                s < sums_end - 1,
                summing and s >= last,
                owners[f],
            )
            message = result[0]
            fresh = result[-1] if summing and s >= last else None
            act[f] = fresh
            if carries:
                held[o][s - first] = message
            if s < sums_end - 1 or (carries and s < first + chunks + last - 1):
                got[f] = lax.ppermute(message, ("dp", "expert"), flows[f])
            if f == 0:
                climbing = message
            else:
                for j in range(1, experts):
                    if max(0, order.index((j, 0)) - 2) == s:
                        rows[j] = rows_for(j, message[:1, :1])
            if f == 0 and carries:
                outs.append(lower(m, held[0][s - first], message, wd))
        if s + 1 < sums_end:
            partial = project(round_rows(s + 1), wg, wu, (climbing,))

    def across(part):
        if tensors == 2:
            other = lax.ppermute(part, "tensor", [(0, 1), (1, 0)])
            return (part.astype(F32) + other.astype(F32)).astype(BF16)
        return lax.psum(part, "tensor")

    def finished(start, stop):
        return [
            jnp.concatenate(
                [
                    pick([outs[c + a][f * m : (f + 1) * m] for a in range(depth)], spot[1 - f])
                    for c in range(start, stop)
                ]
            )
            for f in range(2)
        ]

    yields = [jnp.zeros((n, width), F32), jnp.zeros((n, width), F32)]
    spans = []
    for index, (j, i) in enumerate(order):
        if spans and spans[-1][0] == j:
            spans[-1][2] = index + 1
        else:
            spans.append([j, index, index + 1, i])
    for j, start, stop, i in spans:
        size = (stop - start) * m
        part = across(jnp.concatenate(finished(start, stop)))
        if j:
            part = lax.ppermute(part, "expert", [(a, a ^ j) for a in range(experts)])
        ranks = jnp.arange(size, dtype=jnp.int32) + i * m
        ranks = jnp.concatenate([ranks, ranks + half])
        label = ranks * experts + (e ^ j)
        for k in range(2):
            chosen = (label[:, None] == places[k][None, :]).astype(BF16)
            yields[k] += lax.dot_general(
                chosen, part, (((0,), (0,)), ((), ())), preferred_element_type=F32
            )
    mixed = gates[:, 0:1] * yields[0] + gates[:, 1:2] * yields[1]
    return mixed.astype(BF16)


def solution(mesh):
    return jax.shard_map(
        local,
        mesh=mesh,
        in_specs=(
            P("expert", "dp"),
            P("expert", None),
            P("expert", None),
            P("expert", "dp", "tensor"),
            P("expert", "dp", "tensor"),
            P("expert", "tensor", "dp"),
        ),
        out_specs=P("expert", "dp"),
        check_vma=False,
    )
```

```python
import jax
import jax.numpy as jnp
from jax import lax
from jax.experimental import pallas as pl
from jax.experimental.pallas import tpu as pltpu
from jax.sharding import PartitionSpec as P

F32, BF16, I32 = jnp.float32, jnp.bfloat16, jnp.int32
CHUNK = 32
WHOLE = pl.BlockSpec(memory_space=pltpu.VMEM)
SCALAR = pl.BlockSpec(memory_space=pltpu.SMEM)
FAR = pl.BlockSpec(memory_space=pltpu.HBM)
LIGHT = pl.CostEstimate(flops=0, bytes_accessed=0, transcendentals=0)


def chunk_order(experts, per):
    head = max(1, per // 2)
    order = [(0, i) for i in range(head)]
    order += [(j, i) for j in range(1, experts) for i in range(per)]
    return order + [(0, i) for i in range(head, per)]


def pick(options, index):
    out = options[-1]
    for k in range(len(options) - 2, -1, -1):
        out = jnp.where(index == k, options[k], out)
    return out


def array(*shape, dtype=BF16):
    return jax.ShapeDtypeStruct(shape, dtype)


def call(body, name, shapes, args, specs=None, scratch=(), grant=16):
    if specs is None:
        specs = [SCALAR if a.dtype == I32 else WHOLE for a in args]
    return pl.pallas_call(
        body,
        name=name,
        out_shape=shapes,
        in_specs=specs,
        out_specs=[WHOLE] * len(shapes),
        scratch_shapes=scratch,
        cost_estimate=LIGHT,
        compiler_params=pltpu.CompilerParams(vmem_limit_bytes=grant * 2**20),
    )(*args)


def tiles_of(columns, wide):
    wide = wide if columns % wide == 0 else columns
    return [pl.ds(at, wide) for at in range(0, columns, wide)]


def one_hot(mask):
    return jnp.where(mask, 1.0, 0.0).astype(BF16)


def begin(m, experts, capacity, e, ids, tokens, wg, wu):
    n, width = tokens.shape
    units = wg.shape[1]
    half = capacity // 2
    cuts = tiles_of(units, 512)
    names = (experts + 15) // 16 * 16

    def body(e_ref, ids_hbm, tok_hbm, wg_hbm, wu_hbm, place_ref, *rest):
        rows = rest[:experts]
        wg_ref, wu_ref, g_ref, u_ref, x_ref, ids_ref, tok_ref, sems, small = rest[experts:]
        ids_copy = pltpu.make_async_copy(ids_hbm, ids_ref, small.at[0])
        tok_copy = pltpu.make_async_copy(tok_hbm, tok_ref, small.at[1])
        ids_copy.start()
        tok_copy.start()
        pairs = ((wg_hbm, wg_ref, g_ref), (wu_hbm, wu_ref, u_ref))

        def load(k, t):
            return pltpu.make_async_copy(
                pairs[k][0].at[:, cuts[t]], pairs[k][1].at[:, cuts[t]], sems.at[k, t]
            )

        for t in range(len(cuts)):
            for k in range(2):
                load(k, t).start()
        ids_copy.wait()
        index = lax.broadcasted_iota(I32, (names, n), 0)
        ids = [ids_ref[k : k + 1, :] for k in range(2)]
        hits = [index == ids[k] for k in range(2)]
        earlier = lax.broadcasted_iota(I32, (n, n), 0) < lax.broadcasted_iota(I32, (n, n), 1)
        before = jnp.dot(one_hot(hits[0] | hits[1]), one_hot(earlier), preferred_element_type=F32)
        places = []
        for k in range(2):
            rank = jnp.sum(jnp.where(hits[k], before, 0.0), axis=0, keepdims=True)
            places.append(rank.astype(I32) * experts + ids[k])
            place_ref[k : k + 1, :] = places[k]
        lines = lax.broadcasted_iota(I32, (capacity, n), 0) * experts
        tok_copy.wait()
        for j in range(experts):
            mine = lines + (e_ref[0] ^ j)
            chosen = one_hot((mine == places[0]) | (mine == places[1]))
            picked = jnp.dot(chosen, tok_ref[...], preferred_element_type=F32).astype(BF16)
            rows[j][...] = picked
            if j == 0:
                x_ref[:m] = picked[:m]
                x_ref[m:] = picked[half : half + m]
        for t in range(len(cuts)):
            for k in range(2):
                load(k, t).wait()
                pairs[k][2][:, cuts[t]] = jnp.dot(
                    x_ref[...], pairs[k][1][:, cuts[t]], preferred_element_type=F32
                ).astype(BF16)

    shapes = [array(2, n, dtype=I32)] + [array(capacity, width)] * experts
    shapes += [array(width, units)] * 2 + [array(2 * m, units)] * 2
    out = call(
        body,
        "begin",
        shapes,
        (e, ids, tokens, wg, wu),
        [SCALAR, FAR, FAR, FAR, FAR],
        [
            pltpu.VMEM((2 * m, width), BF16),
            pltpu.VMEM((2, n), I32),
            pltpu.VMEM((n, width), BF16),
            pltpu.SemaphoreType.DMA((2, len(cuts))),
            pltpu.SemaphoreType.DMA((2,)),
        ],
        grant=36,
    )
    return out[0], out[1 : 1 + experts], out[1 + experts : 3 + experts], out[3 + experts :]


def project(m, spots, rows, sources, weights, tie):
    used = sorted({c[0] for per_flow in sources for c in per_flow if c})
    width, units = weights[0].shape

    def body(spot_ref, *refs):
        groups = dict(zip(used, refs))
        wg_ref, wu_ref = refs[len(used) : len(used) + 2]
        g_ref, u_ref, x_ref = refs[-3:]
        for f in range(2):
            options = [
                jnp.zeros((m, width), BF16) if c is None else groups[c[0]][c[1] : c[1] + m, :]
                for c in sources[f]
            ]
            x_ref[f * m : (f + 1) * m] = pick(options, spot_ref[f])
        for cols in tiles_of(units, 1024):
            for w_ref, out_ref in ((wg_ref, g_ref), (wu_ref, u_ref)):
                out_ref[:, cols] = jnp.dot(
                    x_ref[...], w_ref[:, cols], preferred_element_type=F32
                ).astype(BF16)

    return call(
        body,
        "project",
        [array(2 * m, units)] * 2,
        (spots, *(rows[j] for j in used), *weights, tie),
        scratch=[pltpu.VMEM((2 * m, width), BF16)],
    )


def combine(m, units, f, first, came, partial, act, summing, sending, fresh, spots, ties, relay):
    args, use = [], {}

    def take(key, value):
        if value is not None:
            use[key] = len(args)
            args.append(value)

    take("spots", spots if act is not None and came is not None else None)
    take("came", came)
    if summing:
        take("g", partial[0])
        take("u", partial[1])
    take("act", act)
    take("relay", relay)
    taken = len(args)
    args += ties
    sums = 2 * m if summing and sending else 0
    hidden = act is not None or (came is not None and came.shape[0] % (2 * m) == m)
    rows = sums + (m if hidden else 0)
    shapes = [array(rows, units)] if rows else []
    if fresh:
        shapes.append(array(m, units))
    if relay is not None:
        shapes.append(array(*relay.shape))

    def body(*refs):
        ins, outs = refs[:taken], refs[len(args) :]
        ref = {key: ins[at] for key, at in use.items()}
        if relay is not None:
            outs[-1][...] = ref["relay"][...]

        def step(cols):
            if summing:
                total = []
                for k, key in enumerate(("g", "u")):
                    value = ref[key][f * m : (f + 1) * m, cols].astype(F32)
                    if not first:
                        value = value + ref["came"][k * m : (k + 1) * m, cols].astype(F32)
                    total.append(value)
                    if sending:
                        outs[0][k * m : (k + 1) * m, cols] = value.astype(BF16)
                if fresh:
                    g, u = total
                    outs[1 if rows else 0][:, cols] = (g / (1.0 + jnp.exp(-g)) * u).astype(BF16)
            if hidden:
                if "came" in ref and came.shape[0] % (2 * m) == m:
                    h = ref["came"][came.shape[0] - m :, cols]
                    if "act" in ref:
                        h = jnp.where(ref["spots"][f] == 0, ref["act"][:, cols], h)
                else:
                    h = ref["act"][:, cols]
                outs[0][sums:, cols] = h

        wide = 512 if units % 512 == 0 else units

        def loop(i, carry):
            step(pl.ds(pl.multiple_of(i * wide, wide), wide))
            return carry

        lax.fori_loop(0, units // wide, loop, 0)

    out = list(call(body, "combine", shapes, args))
    relayed = out.pop() if relay is not None else None
    activated = out.pop() if fresh else None
    return (out[0] if rows else None), activated, relayed


def lower(m, one, two, wd, tie):
    columns = wd.shape[1]

    def body(one_ref, two_ref, w_ref, *rest):
        h = jnp.concatenate([r[r.shape[0] - m :, :] for r in (one_ref, two_ref)])
        for cols in tiles_of(columns, 256):
            rest[-1][:, cols] = jnp.dot(h, w_ref[:, cols], preferred_element_type=F32).astype(BF16)

    return call(body, "lower", [array(2 * m, columns)], (one, two, wd, *tie))[0]


def local(tokens, route_ids, gates, w_gate, w_up, w_down):
    experts = lax.axis_size("expert")
    depth = lax.axis_size("dp")
    tensors = lax.axis_size("tensor")
    z = lax.axis_index("dp")
    e = lax.axis_index("expert")
    n, width = tokens.shape
    units = w_gate.shape[2]
    capacity = max(3 * n // 8, 2 * n // experts)
    capacity = (capacity + 15) // 16 * 16
    half = capacity // 2
    m = CHUNK if half % CHUNK == 0 else 16
    per = half // m
    order = chunk_order(experts, per)
    chunks = len(order)
    last = depth - 1

    even = e % 2 == 0
    spot = [jnp.where(even, z, last - z), jnp.where(even, last - z, z)]
    spots = jnp.stack(spot).astype(I32)
    climb = [(a * experts + b, (a + 1) * experts + b) for a in range(last) for b in range(experts)]
    flows = [[(a, c) if a % experts % 2 == f else (c, a) for a, c in climb] for f in range(2)]

    places, picked, weights, partial = begin(
        m, experts, capacity, e.astype(I32).reshape(1), route_ids.T, tokens, w_gate[0], w_up[0]
    )
    rows = [picked[0]] + [None] * (experts - 1)
    due = {max(0, order.index((j, 0)) - 2): j for j in range(1, experts)}

    def sources(s):
        found = [[None] * depth for _ in range(2)]
        for f in range(2):
            for a in range(depth):
                if 0 <= s - a < chunks:
                    j, i = order[s - a]
                    found[f][a] = (j, f * half + i * m)
        return found

    wd = w_down[0]
    sums_end = chunks + last
    got = [None, None]
    act = [None, None]
    held = [{}, {}]
    outs = []
    ties = []
    for s in range(chunks + 2 * last + 1):
        summing = s < sums_end
        following = None
        for f in range(2):
            o = 1 - f
            first = last + 1 if f == 0 else last
            carries = first <= s < first + chunks + last
            if not (summing or carries):
                continue
            message, act[f], relayed = combine(
                m,
                units,
                f,
                s == 0,
                got[f] if s else None,
                partial,
                act[o] if carries else None,
                summing,
                s < sums_end - 1,
                summing and s >= last,
                spots,
                ties,
                picked[due[s]] if f == 1 and s in due else None,
            )
            ties = []
            if s < sums_end - 1 or (carries and s < first + chunks + last - 1):
                got[f] = lax.ppermute(message, ("dp", "expert"), flows[f])
            if relayed is not None:
                j = due[s]
                rows[j] = lax.ppermute(relayed, "expert", [(a, a ^ j) for a in range(experts)])
            if carries:
                held[o][s - first] = message
            if f == 0 and s + 1 < sums_end and all(
                rows[c[0]] is not None for per_flow in sources(s + 1) for c in per_flow if c
            ):
                following = project(m, spots, rows, sources(s + 1), weights, message)
                ties.append(following[0])
            if f == 1 and s + 1 < sums_end and following is None:
                following = project(m, spots, rows, sources(s + 1), weights, message)
                ties.append(following[0])
            if f == 1 and s - last - 1 in held[1]:
                q = s - last - 1
                outs.append(lower(m, held[0][q], held[1][q], wd, (message,)))
                ties.append(outs[-1])
            if f == 0 and carries and s == chunks + 2 * last:
                q = s - last - 1
                outs.append(lower(m, held[0][q], held[1][q], wd, ()))
        partial = following

    def finished(start, stop):
        return [
            jnp.concatenate(
                [
                    pick([outs[c + a][f * m : (f + 1) * m] for a in range(depth)], spot[1 - f])
                    for c in range(start, stop)
                ]
            )
            for f in range(2)
        ]

    yields = [jnp.zeros((n, width), F32), jnp.zeros((n, width), F32)]
    spans = []
    for index, (j, i) in enumerate(order):
        if spans and spans[-1][0] == j:
            spans[-1][2] = index + 1
        else:
            spans.append([j, index, index + 1, i])
    for j, start, stop, i in spans:
        size = (stop - start) * m
        part = jnp.concatenate(finished(start, stop))
        if tensors == 2 and stop >= chunks - 1:
            other = lax.ppermute(part, "tensor", [(0, 1), (1, 0)])
            part = (part.astype(F32) + other.astype(F32)).astype(BF16)
        else:
            part = lax.psum(part, "tensor")
        if j:
            part = lax.ppermute(part, "expert", [(a, a ^ j) for a in range(experts)])
        ranks = jnp.arange(size, dtype=I32) + i * m
        ranks = jnp.concatenate([ranks, ranks + half])
        label = ranks * experts + (e ^ j)
        for k in range(2):
            chosen = (label[:, None] == places[k][None, :]).astype(BF16)
            yields[k] += lax.dot_general(
                chosen, part, (((0,), (0,)), ((), ())), preferred_element_type=F32
            )
    mixed = gates[:, 0:1] * yields[0] + gates[:, 1:2] * yields[1]
    return mixed.astype(BF16)


def solution(mesh):
    return jax.shard_map(
        local,
        mesh=mesh,
        in_specs=(
            P("expert", "dp"),
            P("expert", None),
            P("expert", None),
            P("expert", "dp", "tensor"),
            P("expert", "dp", "tensor"),
            P("expert", "tensor", "dp"),
        ),
        out_specs=P("expert", "dp"),
        check_vma=False,
    )
```

```python
import jax
import jax.numpy as jnp
from jax import lax
from jax.experimental import pallas as pl
from jax.experimental.pallas import tpu as pltpu
from jax.sharding import PartitionSpec as P

F32, BF16, I32 = jnp.float32, jnp.bfloat16, jnp.int32
CHUNK = 32
WHOLE = pl.BlockSpec(memory_space=pltpu.VMEM)
SCALAR = pl.BlockSpec(memory_space=pltpu.SMEM)
FAR = pl.BlockSpec(memory_space=pltpu.HBM)
LIGHT = pl.CostEstimate(flops=0, bytes_accessed=0, transcendentals=0)


def chunk_order(experts, per):
    head = max(1, per // 2)
    order = [(0, i) for i in range(head)]
    order += [(j, i) for j in range(1, experts) for i in range(per)]
    return order + [(0, i) for i in range(head, per)]


def pick(options, index):
    out = options[-1]
    for k in range(len(options) - 2, -1, -1):
        out = jnp.where(index == k, options[k], out)
    return out


def array(*shape, dtype=BF16):
    return jax.ShapeDtypeStruct(shape, dtype)


def call(body, name, shapes, args, specs=None, scratch=(), grant=16):
    if specs is None:
        specs = [SCALAR if a.dtype == I32 else WHOLE for a in args]
    return pl.pallas_call(
        body,
        name=name,
        out_shape=shapes,
        in_specs=specs,
        out_specs=[WHOLE] * len(shapes),
        scratch_shapes=scratch,
        cost_estimate=LIGHT,
        compiler_params=pltpu.CompilerParams(vmem_limit_bytes=grant * 2**20),
    )(*args)


def tiles_of(columns, wide):
    wide = wide if columns % wide == 0 else columns
    return [pl.ds(at, wide) for at in range(0, columns, wide)]


def one_hot(mask):
    return jnp.where(mask, 1.0, 0.0).astype(BF16)


def streamed(pieces, buffers, sems, use):
    slots = buffers.shape[0]

    def load(i):
        return pltpu.make_async_copy(pieces[i], buffers.at[i % slots], sems.at[i % slots])

    for i in range(min(slots, len(pieces))):
        load(i).start()

    def run(i):
        load(i).wait()
        use(i, buffers.at[i % slots])
        if i + slots < len(pieces):
            load(i + slots).start()

    return run


def begin(m, experts, capacity, e, ids, tokens, wg, wu):
    n, width = tokens.shape
    units = wg.shape[1]
    half = capacity // 2
    cuts = tiles_of(units, 512)
    names = (experts + 15) // 16 * 16

    def body(e_ref, ids_hbm, tok_hbm, wg_hbm, wu_hbm, place_ref, *rest):
        rows = rest[:experts]
        g_ref, u_ref, x_ref, ids_ref, tok_ref, buffers, sems, small = rest[experts:]
        ids_copy = pltpu.make_async_copy(ids_hbm, ids_ref, small.at[0])
        tok_copy = pltpu.make_async_copy(tok_hbm, tok_ref, small.at[1])
        ids_copy.start()
        tok_copy.start()

        def use(i, w_ref):
            (g_ref, u_ref)[i % 2][:, cuts[i // 2]] = jnp.dot(
                x_ref[...], w_ref[...], preferred_element_type=F32
            ).astype(BF16)

        pieces = [w.at[:, c] for c in cuts for w in (wg_hbm, wu_hbm)]
        run = streamed(pieces, buffers, sems, use)
        ids_copy.wait()
        index = lax.broadcasted_iota(I32, (names, n), 0)
        ids = [ids_ref[k : k + 1, :] for k in range(2)]
        hits = [index == ids[k] for k in range(2)]
        earlier = lax.broadcasted_iota(I32, (n, n), 0) < lax.broadcasted_iota(I32, (n, n), 1)
        before = jnp.dot(one_hot(hits[0] | hits[1]), one_hot(earlier), preferred_element_type=F32)
        places = []
        for k in range(2):
            rank = jnp.sum(jnp.where(hits[k], before, 0.0), axis=0, keepdims=True)
            places.append(rank.astype(I32) * experts + ids[k])
            place_ref[k : k + 1, :] = places[k]
        lines = lax.broadcasted_iota(I32, (capacity, n), 0) * experts
        tok_copy.wait()
        for j in range(experts):
            mine = lines + (e_ref[0] ^ j)
            chosen = one_hot((mine == places[0]) | (mine == places[1]))
            picked = jnp.dot(chosen, tok_ref[...], preferred_element_type=F32).astype(BF16)
            rows[j][...] = picked
            if j == 0:
                x_ref[:m] = picked[:m]
                x_ref[m:] = picked[half : half + m]
        for i in range(len(pieces)):
            run(i)

    shapes = [array(2, n, dtype=I32)] + [array(capacity, width)] * experts
    shapes += [array(2 * m, units)] * 2
    slots = 2 * len(cuts)
    out = call(
        body,
        "begin",
        shapes,
        (e, ids, tokens, wg, wu),
        [SCALAR, FAR, FAR, FAR, FAR],
        [
            pltpu.VMEM((2 * m, width), BF16),
            pltpu.VMEM((2, n), I32),
            pltpu.VMEM((n, width), BF16),
            pltpu.VMEM((slots, width, units // len(cuts)), BF16),
            pltpu.SemaphoreType.DMA((slots,)),
            pltpu.SemaphoreType.DMA((2,)),
        ],
        grant=48,
    )
    return out[0], out[1 : 1 + experts], out[1 + experts :]


def project(m, spot, rows, plans, weights, tie):
    used = sorted({c[0] for plan in plans for per_flow in plan for c in per_flow if c})
    width, units = weights[0].shape
    total = 2 * m * len(plans)
    cuts = tiles_of(units, 512)

    def body(spot0_ref, spot1_ref, *refs):
        groups = dict(zip(used, refs))
        w_hbm = refs[len(used) : len(used) + 2]
        g_ref, u_ref, x_ref, buffers, sems = refs[-5:]

        def use(i, w_ref):
            (g_ref, u_ref)[i % 2][:, cuts[i // 2]] = jnp.dot(
                x_ref[...], w_ref[...], preferred_element_type=F32
            ).astype(BF16)

        pieces = [w.at[:, c] for c in cuts for w in w_hbm]
        run = streamed(pieces, buffers, sems, use)
        for r, plan in enumerate(plans):
            for f in range(2):
                options = [
                    jnp.zeros((m, width), BF16) if c is None else groups[c[0]][c[1] : c[1] + m, :]
                    for c in plan[f]
                ]
                at = (2 * r + f) * m
                x_ref[at : at + m] = pick(options, (spot0_ref, spot1_ref)[f][0])
        for i in range(len(pieces)):
            run(i)

    args = (*spot, *(rows[j] for j in used), *weights, tie)
    slots = min(8, 2 * len(cuts))
    return call(
        body,
        "project",
        [array(total, units)] * 2,
        args,
        [SCALAR] * 2 + [WHOLE] * len(used) + [FAR] * 2 + [WHOLE],
        [
            pltpu.VMEM((total, width), BF16),
            pltpu.VMEM((slots, width, units // len(cuts)), BF16),
            pltpu.SemaphoreType.DMA((slots,)),
        ],
        grant=48,
    )


def combine(m, units, f, first, came, partial, act, summing, sending, fresh, spot, ties, relay):
    args, use = [], {}

    def take(key, value):
        if value is not None:
            use[key] = len(args)
            args.append(value)

    take("spot", spot if act is not None and came is not None else None)
    take("came", came)
    if summing:
        take("g", partial[0])
        take("u", partial[1])
        base = partial[2] + f * m
    take("act", act)
    take("relay", relay)
    taken = len(args)
    args += ties
    sums = 2 * m if summing and sending else 0
    hidden = act is not None or (came is not None and came.shape[0] % (2 * m) == m)
    rows = sums + (m if hidden else 0)
    shapes = [array(rows, units)] if rows else []
    if fresh:
        shapes.append(array(m, units))
    if relay is not None:
        shapes.append(array(*relay.shape))

    def body(*refs):
        ins, outs = refs[:taken], refs[len(args) :]
        ref = {key: ins[at] for key, at in use.items()}
        if relay is not None:
            outs[-1][...] = ref["relay"][...]

        def step(cols):
            if summing:
                total = []
                for k, key in enumerate(("g", "u")):
                    value = ref[key][base : base + m, cols].astype(F32)
                    if not first:
                        value = value + ref["came"][k * m : (k + 1) * m, cols].astype(F32)
                    total.append(value)
                    if sending:
                        outs[0][k * m : (k + 1) * m, cols] = value.astype(BF16)
                if fresh:
                    g, u = total
                    outs[1 if rows else 0][:, cols] = (g / (1.0 + jnp.exp(-g)) * u).astype(BF16)
            if hidden:
                if "came" in ref and came.shape[0] % (2 * m) == m:
                    h = ref["came"][came.shape[0] - m :, cols]
                    if "act" in ref:
                        h = jnp.where(ref["spot"][0] == 0, ref["act"][:, cols], h)
                else:
                    h = ref["act"][:, cols]
                outs[0][sums:, cols] = h

        wide = 512 if units % 512 == 0 else units

        def loop(i, carry):
            step(pl.ds(pl.multiple_of(i * wide, wide), wide))
            return carry

        lax.fori_loop(0, units // wide, loop, 0)

    out = list(call(body, "combine", shapes, args))
    relayed = out.pop() if relay is not None else None
    activated = out.pop() if fresh else None
    return (out[0] if rows else None), activated, relayed


def lower(m, pairs, wd, tie):
    units, columns = wd.shape
    total = 2 * m * len(pairs)
    cuts = tiles_of(units, 512)
    flat = [message for pair in pairs for message in pair]

    def body(*refs):
        messages, w_hbm = refs[: len(flat)], refs[len(flat)]
        out_ref, sum_ref, buffers, sems = refs[-4:]

        def use(i, w_ref):
            h = jnp.concatenate([r[r.shape[0] - m :, cuts[i]] for r in messages])
            part = jnp.dot(h, w_ref[...], preferred_element_type=F32)
            if i:
                part = part + sum_ref[...]
            if i == len(cuts) - 1:
                out_ref[...] = part.astype(BF16)
            else:
                sum_ref[...] = part

        run = streamed([w_hbm.at[c, :] for c in cuts], buffers, sems, use)
        for i in range(len(cuts)):
            run(i)

    slots = min(6, len(cuts))
    return call(
        body,
        "lower",
        [array(total, columns)],
        (*flat, wd, *tie),
        [WHOLE] * len(flat) + [FAR] + [WHOLE] * len(tie),
        [
            pltpu.VMEM((total, columns), F32),
            pltpu.VMEM((slots, units // len(cuts), columns), BF16),
            pltpu.SemaphoreType.DMA((slots,)),
        ],
        grant=48,
    )[0]


def local(tokens, route_ids, gates, w_gate, w_up, w_down):
    experts = lax.axis_size("expert")
    depth = lax.axis_size("dp")
    tensors = lax.axis_size("tensor")
    z = lax.axis_index("dp")
    e = lax.axis_index("expert")
    n, width = tokens.shape
    units = w_gate.shape[2]
    capacity = max(3 * n // 8, 2 * n // experts)
    capacity = (capacity + 15) // 16 * 16
    half = capacity // 2
    m = CHUNK if half % CHUNK == 0 else 16
    per = half // m
    order = chunk_order(experts, per)
    chunks = len(order)
    last = depth - 1

    even = e % 2 == 0
    spot = [jnp.where(even, z, last - z), jnp.where(even, last - z, z)]
    spot = [a.astype(I32).reshape(1) for a in spot]
    climb = [(a * experts + b, (a + 1) * experts + b) for a in range(last) for b in range(experts)]
    flows = [[(a, c) if a % experts % 2 == f else (c, a) for a, c in climb] for f in range(2)]

    weights = (w_gate[0], w_up[0])
    places, picked, opening = begin(
        m, experts, capacity, e.astype(I32).reshape(1), route_ids.T, tokens, *weights
    )
    rows = [picked[0]] + [None] * (experts - 1)
    due = {max(0, order.index((j, 0)) - 2): j for j in range(1, experts)}

    def sources(s):
        found = [[None] * depth for _ in range(2)]
        for f in range(2):
            for a in range(depth):
                if 0 <= s - a < chunks:
                    j, i = order[s - a]
                    found[f][a] = (j, f * half + i * m)
        return found

    wd = w_down[0]
    sums_end = chunks + last
    ticks = chunks + 2 * last + 1
    partial = {0: (*opening, 0)}
    got = [None, None]
    act = [None, None]
    held = [{}, {}]
    outs = {}
    ties = []
    for s in range(ticks):
        summing = s < sums_end
        for f in (0, 1):
            o = 1 - f
            first = last + 1 if f == 0 else last
            carries = first <= s < first + chunks + last
            if not (summing or carries):
                continue
            message, act[f], relayed = combine(
                m,
                units,
                f,
                s == 0,
                got[f] if s else None,
                partial.get(s),
                act[o] if carries else None,
                summing,
                s < sums_end - 1,
                summing and s >= last,
                spot[f],
                ties,
                picked[due[s]] if f == 1 and s in due else None,
            )
            ties = []
            if s < sums_end - 1 or (carries and s < first + chunks + last - 1):
                got[f] = lax.ppermute(message, ("dp", "expert"), flows[f])
            if relayed is not None:
                j = due[s]
                rows[j] = lax.ppermute(relayed, "expert", [(a, a ^ j) for a in range(experts)])
            if carries:
                held[o][s - first] = message
            if f == 1 and s + 1 < sums_end and s + 1 not in partial:
                rounds = [r for r in (s + 1, s + 2) if r < sums_end]
                g, u = project(m, spot, rows, [sources(r) for r in rounds], weights, message)
                for k, r in enumerate(rounds):
                    partial[r] = (g, u, 2 * m * k)
                ties = [g]
            if f == 1 or s == ticks - 1:
                ready = [q for q in range(chunks + last) if q in held[0] and q in held[1]]
                ready = [q for q in ready if q not in outs]
                if len(ready) == 2 or (ready and ready[0] >= chunks):
                    tie = () if s == ticks - 1 else (message,)
                    pairs = [(held[0][q], held[1][q]) for q in ready]
                    result = lower(m, pairs, wd, tie)
                    for k, q in enumerate(ready):
                        outs[q] = result[2 * m * k : 2 * m * (k + 1)]
                    ties = ties + [result]

    def finished(start, stop):
        return [
            jnp.concatenate(
                [
                    pick([outs[c + a][f * m : (f + 1) * m] for a in range(depth)], spot[1 - f][0])
                    for c in range(start, stop)
                ]
            )
            for f in range(2)
        ]

    yields = [jnp.zeros((n, width), F32), jnp.zeros((n, width), F32)]
    spans = []
    for index, (j, i) in enumerate(order):
        if spans and spans[-1][0] == j:
            spans[-1][2] = index + 1
        else:
            spans.append([j, index, index + 1, i])
    for j, start, stop, i in spans:
        size = (stop - start) * m
        part = jnp.concatenate(finished(start, stop))
        if tensors == 2:
            other = lax.ppermute(part, "tensor", [(0, 1), (1, 0)])
            part = (part.astype(F32) + other.astype(F32)).astype(BF16)
        else:
            part = lax.psum(part, "tensor")
        if j:
            part = lax.ppermute(part, "expert", [(a, a ^ j) for a in range(experts)])
        ranks = jnp.arange(size, dtype=I32) + i * m
        ranks = jnp.concatenate([ranks, ranks + half])
        label = ranks * experts + (e ^ j)
        for k in range(2):
            chosen = (label[:, None] == places[k][None, :]).astype(BF16)
            yields[k] += lax.dot_general(
                chosen, part, (((0,), (0,)), ((), ())), preferred_element_type=F32
            )
    mixed = gates[:, 0:1] * yields[0] + gates[:, 1:2] * yields[1]
    return mixed.astype(BF16)


def solution(mesh):
    return jax.shard_map(
        local,
        mesh=mesh,
        in_specs=(
            P("expert", "dp"),
            P("expert", None),
            P("expert", None),
            P("expert", "dp", "tensor"),
            P("expert", "dp", "tensor"),
            P("expert", "tensor", "dp"),
        ),
        out_specs=P("expert", "dp"),
        check_vma=False,
    )
```

```python
import jax
import jax.numpy as jnp
import numpy as np
from jax import lax
from jax.experimental import pallas as pl
from jax.experimental.pallas import tpu as pltpu
from jax.sharding import PartitionSpec as P

F32, BF16, I32 = jnp.float32, jnp.bfloat16, jnp.int32
CHUNK = 32
WHOLE = pl.BlockSpec(memory_space=pltpu.VMEM)
SCALAR = pl.BlockSpec(memory_space=pltpu.SMEM)
FAR = pl.BlockSpec(memory_space=pltpu.HBM)
LIGHT = pl.CostEstimate(flops=0, bytes_accessed=0, transcendentals=0)


def chunk_order(experts, per):
    head = max(1, per // 2)
    order = [(0, i) for i in range(head)]
    order += [(j, i) for j in range(1, experts) for i in range(per)]
    return order + [(0, i) for i in range(head, per)]


def pick(options, index):
    out = options[-1]
    for k in range(len(options) - 2, -1, -1):
        out = jnp.where(index == k, options[k], out)
    return out


def array(*shape, dtype=BF16):
    return jax.ShapeDtypeStruct(shape, dtype)


def call(body, name, shapes, args, specs=None, scratch=(), grant=16):
    if specs is None:
        specs = [SCALAR if a.dtype == I32 else WHOLE for a in args]
    return pl.pallas_call(
        body,
        name=name,
        out_shape=shapes,
        in_specs=specs,
        out_specs=[WHOLE] * len(shapes),
        scratch_shapes=scratch,
        cost_estimate=LIGHT,
        compiler_params=pltpu.CompilerParams(vmem_limit_bytes=grant * 2**20),
    )(*args)


def tiles_of(columns, wide):
    wide = wide if columns % wide == 0 else columns
    return [pl.ds(at, wide) for at in range(0, columns, wide)]


def one_hot(mask):
    return jnp.where(mask, 1.0, 0.0).astype(BF16)


def streamed(pieces, buffers, sems, use):
    slots = buffers.shape[0]

    def load(i):
        return pltpu.make_async_copy(pieces[i], buffers.at[i % slots], sems.at[i % slots])

    for i in range(min(slots, len(pieces))):
        load(i).start()

    def run(i):
        load(i).wait()
        use(i, buffers.at[i % slots])
        if i + slots < len(pieces):
            load(i + slots).start()

    return run


def begin(m, experts, capacity, e, spot, ids, tokens, wg, wu):
    n, width = tokens.shape
    units = wg.shape[1]
    half = capacity // 2
    cuts = tiles_of(units, 512)
    names = (experts + 15) // 16 * 16

    def body(e_ref, spot0_ref, spot1_ref, ids_hbm, tok_hbm, wg_hbm, wu_hbm, place_ref, *rest):
        rows = rest[:experts]
        mark_ref, g_ref, u_ref, x_ref, ids_ref, tok_ref, buffers, sems, small = rest[experts:]
        ids_copy = pltpu.make_async_copy(ids_hbm, ids_ref, small.at[0])
        tok_copy = pltpu.make_async_copy(tok_hbm, tok_ref, small.at[1])
        ids_copy.start()
        tok_copy.start()

        def use(i, w_ref):
            (g_ref, u_ref)[i % 2][:, cuts[i // 2]] = jnp.dot(
                x_ref[...], w_ref[...], preferred_element_type=F32
            ).astype(BF16)

        pieces = [w.at[:, c] for c in cuts for w in (wg_hbm, wu_hbm)]
        run = streamed(pieces, buffers, sems, use)
        ids_copy.wait()
        index = lax.broadcasted_iota(I32, (names, n), 0)
        ids = [ids_ref[k : k + 1, :] ^ e_ref[0] for k in range(2)]
        mark_ref[:8] = jnp.full((8, 128), spot0_ref[0], I32)
        mark_ref[8:] = jnp.full((8, 128), spot1_ref[0], I32)
        hits = [index == ids[k] for k in range(2)]
        earlier = lax.broadcasted_iota(I32, (n, n), 0) < lax.broadcasted_iota(I32, (n, n), 1)
        before = jnp.dot(one_hot(hits[0] | hits[1]), one_hot(earlier), preferred_element_type=F32)
        places = []
        for k in range(2):
            rank = jnp.sum(jnp.where(hits[k], before, 0.0), axis=0, keepdims=True)
            places.append(rank.astype(I32) * experts + ids[k])
            place_ref[k : k + 1, :] = places[k]
        lines = lax.broadcasted_iota(I32, (capacity, n), 0) * experts
        tok_copy.wait()
        for j in range(experts):
            mine = lines + j
            chosen = one_hot((mine == places[0]) | (mine == places[1]))
            picked = jnp.dot(chosen, tok_ref[...], preferred_element_type=F32).astype(BF16)
            rows[j][...] = picked
            if j == 0:
                x_ref[:m] = picked[:m]
                x_ref[m:] = picked[half : half + m]
        for i in range(len(pieces)):
            run(i)

    shapes = [array(2, n, dtype=I32)] + [array(capacity, width)] * experts
    shapes += [array(16, 128, dtype=I32)] + [array(2 * m, units)] * 2
    slots = 2 * len(cuts)
    out = call(
        body,
        "begin",
        shapes,
        (e, *spot, ids, tokens, wg, wu),
        [SCALAR] * 3 + [FAR] * 4,
        [
            pltpu.VMEM((2 * m, width), BF16),
            pltpu.VMEM((2, n), I32),
            pltpu.VMEM((n, width), BF16),
            pltpu.VMEM((slots, width, units // len(cuts)), BF16),
            pltpu.SemaphoreType.DMA((slots,)),
            pltpu.SemaphoreType.DMA((2,)),
        ],
        grant=48,
    )
    return out[0], out[1 : 1 + experts], out[1 + experts], out[2 + experts :]


def project(m, spot, rows, plans, weights, ties):
    used = sorted({c[0] for plan in plans for per_flow in plan for c in per_flow if c})
    width, units = weights[0].shape
    total = 2 * m * len(plans)
    cuts = tiles_of(units, 512)

    def body(spot0_ref, spot1_ref, *refs):
        groups = dict(zip(used, refs))
        w_hbm = refs[len(used) : len(used) + 2]
        g_ref, u_ref, x_ref, buffers, sems = refs[-5:]

        def use(i, w_ref):
            (g_ref, u_ref)[i % 2][:, cuts[i // 2]] = jnp.dot(
                x_ref[...], w_ref[...], preferred_element_type=F32
            ).astype(BF16)

        pieces = [w.at[:, c] for c in cuts for w in w_hbm]
        run = streamed(pieces, buffers, sems, use)
        for r, plan in enumerate(plans):
            for f in range(2):
                options = [
                    jnp.zeros((m, width), BF16) if c is None else groups[c[0]][c[1] : c[1] + m, :]
                    for c in plan[f]
                ]
                at = (2 * r + f) * m
                x_ref[at : at + m] = pick(options, (spot0_ref, spot1_ref)[f][0])
        for i in range(len(pieces)):
            run(i)

    args = (*spot, *(rows[j] for j in used), *weights, *ties)
    slots = min(8, 2 * len(cuts))
    return call(
        body,
        "project",
        [array(total, units)] * 2,
        args,
        [SCALAR] * 2 + [WHOLE] * len(used) + [FAR] * 2 + [WHOLE] * len(ties),
        [
            pltpu.VMEM((total, width), BF16),
            pltpu.VMEM((slots, width, units // len(cuts)), BF16),
            pltpu.SemaphoreType.DMA((slots,)),
        ],
        grant=48,
    )


def combine(m, units, f, first, came, partial, act, summing, sending, fresh, spot, ties, relay=()):
    args, use = [], {}

    def take(key, value):
        if value is not None:
            use[key] = len(args)
            args.append(value)

    take("spot", spot if act is not None and came is not None else None)
    take("came", came)
    if summing:
        take("g", partial[0])
        take("u", partial[1])
        base = partial[2] + f * m
    take("act", act)
    for k, value in enumerate(relay):
        take(k, value)
    taken = len(args)
    args += ties
    sums = 2 * m if summing and sending else 0
    hidden = act is not None or (came is not None and came.shape[0] % (2 * m) == m)
    rows = sums + (m if hidden else 0)
    shapes = [array(rows, units)] if rows else []
    if fresh:
        shapes.append(array(m, units))
    for value in relay:
        shapes.append(array(*value.shape))

    def body(*refs):
        ins, outs = refs[:taken], refs[len(args) :]
        ref = {key: ins[at] for key, at in use.items()}
        for k in range(len(relay)):
            outs[len(shapes) - len(relay) + k][...] = ref[k][...]

        def step(cols):
            if summing:
                total = []
                for k, key in enumerate(("g", "u")):
                    value = ref[key][base : base + m, cols].astype(F32)
                    if not first:
                        value = value + ref["came"][k * m : (k + 1) * m, cols].astype(F32)
                    total.append(value)
                    if sending:
                        outs[0][k * m : (k + 1) * m, cols] = value.astype(BF16)
                if fresh:
                    g, u = total
                    outs[1 if rows else 0][:, cols] = (g / (1.0 + jnp.exp(-g)) * u).astype(BF16)
            if hidden:
                if "came" in ref and came.shape[0] % (2 * m) == m:
                    h = ref["came"][came.shape[0] - m :, cols]
                    if "act" in ref:
                        h = jnp.where(ref["spot"][0] == 0, ref["act"][:, cols], h)
                else:
                    h = ref["act"][:, cols]
                outs[0][sums:, cols] = h

        wide = 512 if units % 512 == 0 else units

        def loop(i, carry):
            step(pl.ds(pl.multiple_of(i * wide, wide), wide))
            return carry

        lax.fori_loop(0, units // wide, loop, 0)

    out = list(call(body, "combine", shapes, args))
    relayed = [out.pop() for _ in relay][::-1]
    activated = out.pop() if fresh else None
    return (out[0] if rows else None), activated, relayed


def lower(m, pairs, wd, tie):
    units, columns = wd.shape
    total = 2 * m * len(pairs)
    cuts = tiles_of(units, 512)
    flat = [message for pair in pairs for message in pair]

    def body(*refs):
        messages, w_hbm = refs[: len(flat)], refs[len(flat)]
        out_ref, sum_ref, buffers, sems = refs[-4:]

        def use(i, w_ref):
            h = jnp.concatenate([r[r.shape[0] - m :, cuts[i]] for r in messages])
            part = jnp.dot(h, w_ref[...], preferred_element_type=F32)
            if i:
                part = part + sum_ref[...]
            if i == len(cuts) - 1:
                out_ref[...] = part.astype(BF16)
            else:
                sum_ref[...] = part

        run = streamed([w_hbm.at[c, :] for c in cuts], buffers, sems, use)
        for i in range(len(cuts)):
            run(i)

    slots = min(6, len(cuts))
    return call(
        body,
        "lower",
        [array(total, columns)],
        (*flat, wd, *tie),
        [WHOLE] * len(flat) + [FAR] + [WHOLE] * len(tie),
        [
            pltpu.VMEM((total, columns), F32),
            pltpu.VMEM((slots, units // len(cuts), columns), BF16),
            pltpu.SemaphoreType.DMA((slots,)),
        ],
        grant=48,
    )[0]


def local(tokens, route_ids, gates, w_gate, w_up, w_down):
    experts = lax.axis_size("expert")
    depth = lax.axis_size("dp")
    tensors = lax.axis_size("tensor")
    z = lax.axis_index("dp")
    e = lax.axis_index("expert")
    n, width = tokens.shape
    units = w_gate.shape[2]
    capacity = max(3 * n // 8, 2 * n // experts)
    capacity = (capacity + 15) // 16 * 16
    half = capacity // 2
    m = CHUNK if half % CHUNK == 0 else 16
    per = half // m
    order = chunk_order(experts, per)
    chunks = len(order)
    last = depth - 1

    even = e % 2 == 0
    spot = [jnp.where(even, z, last - z), jnp.where(even, last - z, z)]
    spot = [a.astype(I32).reshape(1) for a in spot]
    climb = [(a * experts + b, (a + 1) * experts + b) for a in range(last) for b in range(experts)]
    flows = [[(a, c) if a % experts % 2 == f else (c, a) for a, c in climb] for f in range(2)]

    weights = (w_gate[0], w_up[0])
    wd = w_down[0]
    places, picked, marks, opening = begin(
        m, experts, capacity, e.astype(I32).reshape(1), spot, route_ids.T, tokens, *weights
    )
    rows = [picked[0]]

    def sources(s):
        found = [[None] * depth for _ in range(2)]
        for f in range(2):
            for a in range(depth):
                if 0 <= s - a < chunks:
                    j, i = order[s - a]
                    found[f][a] = (j, f * half + i * m)
        return found

    def across(part):
        if tensors == 2:
            other = lax.ppermute(part, "tensor", [(0, 1), (1, 0)])
            return (part.astype(F32) + other.astype(F32)).astype(BF16)
        return lax.psum(part, "tensor")

    sums_end = chunks + last
    ticks = chunks + 2 * last + 1
    ends = chunks + last
    partial = {0: (*opening, 0)}
    got = [None, None]
    act = [None, None]
    held = [{}, {}]
    outs = {}
    ties = []
    spans = []
    for index, (j, i) in enumerate(order):
        if spans and spans[-1][0] == j:
            spans[-1][2] = index + 1
        else:
            spans.append([j, index, index + 1, i])
    def rounds_of(start, stop):
        return range(start, stop + last)

    def own_copy(start, stop):
        return lax.optimization_barrier([outs[q] for q in rounds_of(start, stop)])

    def finished(start, stop):
        outs = dict(zip(rounds_of(start, stop), own_copy(start, stop)))
        return [
            jnp.concatenate(
                [
                    pick(
                        [outs[c + a][f * m : (f + 1) * m] for a in range(depth)],
                        marks[8 * (1 - f) : 8 * (1 - f) + 1, :1],
                    )
                    for c in range(start, stop)
                ]
            )
            for f in range(2)
        ]

    parts = []

    def deliver():
        for j, start, stop, i in spans[len(parts) :]:
            if all(q in outs for q in rounds_of(start, stop)):
                part = lax.optimization_barrier(jnp.concatenate(finished(start, stop)))
                if j:
                    part = lax.ppermute(part, "expert", [(a, a ^ j) for a in range(experts)])
                parts.append(part)

    for s in range(ticks):
        summing = s < sums_end
        for f in range(2):
            o = 1 - f
            first = last + 1 if f == 0 else last
            carries = first <= s < first + chunks + last
            if not (summing or carries):
                continue
            message, act[f], relayed = combine(
                m,
                units,
                f,
                s == 0,
                got[f] if s else None,
                partial.get(s),
                act[o] if carries else None,
                summing,
                s < sums_end - 1,
                summing and s >= last,
                spot[f],
                ties,
                picked[1:] if s == 0 and f == 1 else (),
            )
            ties = []
            if s < sums_end - 1 or (carries and s < first + chunks + last - 1):
                got[f] = lax.ppermute(message, ("dp", "expert"), flows[f])
            for j, value in enumerate(relayed, 1):
                rows.append(lax.ppermute(value, "expert", [(a, a ^ j) for a in range(experts)]))
            if carries:
                held[o][s - first] = message
            if f == (0 if s else 1) and s + 1 < sums_end and s + 1 not in partial:
                rounds = [r for r in (s + 1, s + 2) if r < sums_end]
                wait = [message] if s else [message, *rows[1:]]
                g, u = project(m, spot, rows, [sources(r) for r in rounds], weights, wait)
                for k, r in enumerate(rounds):
                    partial[r] = (g, u, 2 * m * k)
                ties.append(g)
            ready = [q for q in range(ends) if q in held[0] and q in held[1] and q not in outs]
            if len(ready) == 2 or (ready and ready[0] == ends - 1):
                pairs = [(held[0][q], held[1][q]) for q in ready]
                if ready[0] == ends - 1:
                    deliver()
                result = lower(m, pairs, wd, [message] + (parts if ready[0] == ends - 1 else []))
                ties.append(result)
                result = across(result)
                for k, q in enumerate(ready):
                    outs[q] = result[2 * m * k : 2 * m * (k + 1)]

    yields = [jnp.zeros((n, width), F32), jnp.zeros((n, width), F32)]
    deliver()
    for (j, start, stop, i), part in zip(spans, parts):
        ranks = np.arange((stop - start) * m, dtype=np.int32) + i * m
        label = jnp.asarray(np.concatenate([ranks, ranks + half]) * experts + j)
        for k in range(2):
            chosen = (label[:, None] == places[k][None, :]).astype(BF16)
            yields[k] += lax.dot_general(
                chosen, part, (((0,), (0,)), ((), ())), preferred_element_type=F32
            )
    mixed = gates[:, 0:1] * yields[0] + gates[:, 1:2] * yields[1]
    return mixed.astype(BF16)


def solution(mesh):
    return jax.shard_map(
        local,
        mesh=mesh,
        in_specs=(
            P("expert", "dp"),
            P("expert", None),
            P("expert", None),
            P("expert", "dp", "tensor"),
            P("expert", "dp", "tensor"),
            P("expert", "tensor", "dp"),
        ),
        out_specs=P("expert", "dp"),
        check_vma=False,
    )
```

```python
import jax
import jax.numpy as jnp
import numpy as np
from jax import lax
from jax.experimental import pallas as pl
from jax.experimental.pallas import tpu as pltpu
from jax.sharding import PartitionSpec as P

F32, BF16, I32 = jnp.float32, jnp.bfloat16, jnp.int32
CHUNK = 32
WHOLE = pl.BlockSpec(memory_space=pltpu.VMEM)
SCALAR = pl.BlockSpec(memory_space=pltpu.SMEM)
FAR = pl.BlockSpec(memory_space=pltpu.HBM)
LIGHT = pl.CostEstimate(flops=0, bytes_accessed=0, transcendentals=0)


def chunk_order(experts, per):
    head = max(1, per // 2)
    order = [(0, i) for i in range(head)]
    order += [(j, i) for j in range(1, experts) for i in range(per)]
    return order + [(0, i) for i in range(head, per)]


def pick(options, index):
    out = options[-1]
    for k in range(len(options) - 2, -1, -1):
        out = jnp.where(index == k, options[k], out)
    return out


def array(*shape, dtype=BF16):
    return jax.ShapeDtypeStruct(shape, dtype)


def call(body, name, shapes, args, specs=None, scratch=(), grant=16):
    if specs is None:
        specs = [SCALAR if a.dtype == I32 else WHOLE for a in args]
    return pl.pallas_call(
        body,
        name=name,
        out_shape=shapes,
        in_specs=specs,
        out_specs=[WHOLE] * len(shapes),
        scratch_shapes=scratch,
        cost_estimate=LIGHT,
        compiler_params=pltpu.CompilerParams(vmem_limit_bytes=grant * 2**20),
    )(*args)


def tiles_of(columns, wide):
    wide = wide if columns % wide == 0 else columns
    return [pl.ds(at, wide) for at in range(0, columns, wide)]


def one_hot(mask):
    return jnp.where(mask, 1.0, 0.0).astype(BF16)


def streamed(pieces, buffers, sems, use):
    slots = buffers.shape[0]

    def load(i):
        return pltpu.make_async_copy(pieces[i], buffers.at[i % slots], sems.at[i % slots])

    for i in range(min(slots, len(pieces))):
        load(i).start()

    def run(i):
        load(i).wait()
        use(i, buffers.at[i % slots])
        if i + slots < len(pieces):
            load(i + slots).start()

    return run


def begin(m, experts, capacity, e, spot, ids, tokens, wg, wu):
    n, width = tokens.shape
    units = wg.shape[1]
    half = capacity // 2
    cuts = tiles_of(units, 512)
    names = (experts + 15) // 16 * 16

    def body(e_ref, spot0_ref, spot1_ref, ids_hbm, tok_hbm, wg_hbm, wu_hbm, place_ref, *rest):
        rows = rest[:experts]
        mark_ref, g_ref, u_ref, x_ref, ids_ref, tok_ref, buffers, sems, small = rest[experts:]
        ids_copy = pltpu.make_async_copy(ids_hbm, ids_ref, small.at[0])
        tok_copy = pltpu.make_async_copy(tok_hbm, tok_ref, small.at[1])
        ids_copy.start()
        tok_copy.start()

        def use(i, w_ref):
            (g_ref, u_ref)[i % 2][:, cuts[i // 2]] = jnp.dot(
                x_ref[...], w_ref[...], preferred_element_type=F32
            ).astype(BF16)

        pieces = [w.at[:, c] for c in cuts for w in (wg_hbm, wu_hbm)]
        run = streamed(pieces, buffers, sems, use)
        ids_copy.wait()
        index = lax.broadcasted_iota(I32, (names, n), 0)
        ids = [ids_ref[k : k + 1, :] ^ e_ref[0] for k in range(2)]
        mark_ref[:8] = jnp.full((8, 128), spot0_ref[0], I32)
        mark_ref[8:] = jnp.full((8, 128), spot1_ref[0], I32)
        hits = [index == ids[k] for k in range(2)]
        earlier = lax.broadcasted_iota(I32, (n, n), 0) < lax.broadcasted_iota(I32, (n, n), 1)
        before = jnp.dot(one_hot(hits[0] | hits[1]), one_hot(earlier), preferred_element_type=F32)
        places = []
        for k in range(2):
            rank = jnp.sum(jnp.where(hits[k], before, 0.0), axis=0, keepdims=True)
            places.append(rank.astype(I32) * experts + ids[k])
            place_ref[k : k + 1, :] = places[k]
        lines = lax.broadcasted_iota(I32, (capacity, n), 0) * experts
        tok_copy.wait()
        for j in range(experts):
            mine = lines + j
            chosen = one_hot((mine == places[0]) | (mine == places[1]))
            picked = jnp.dot(chosen, tok_ref[...], preferred_element_type=F32).astype(BF16)
            rows[j][...] = picked
            if j == 0:
                x_ref[:m] = picked[:m]
                x_ref[m:] = picked[half : half + m]
        for i in range(len(pieces)):
            run(i)

    shapes = [array(2, n, dtype=I32)] + [array(capacity, width)] * experts
    shapes += [array(16, 128, dtype=I32)] + [array(2 * m, units)] * 2
    slots = 2 * len(cuts)
    out = call(
        body,
        "begin",
        shapes,
        (e, *spot, ids, tokens, wg, wu),
        [SCALAR] * 3 + [FAR] * 4,
        [
            pltpu.VMEM((2 * m, width), BF16),
            pltpu.VMEM((2, n), I32),
            pltpu.VMEM((n, width), BF16),
            pltpu.VMEM((slots, width, units // len(cuts)), BF16),
            pltpu.SemaphoreType.DMA((slots,)),
            pltpu.SemaphoreType.DMA((2,)),
        ],
        grant=48,
    )
    return out[0], out[1 : 1 + experts], out[1 + experts], out[2 + experts :]


def project(m, spot, rows, plans, weights, ties):
    used = sorted({c[0] for plan in plans for per_flow in plan for c in per_flow if c})
    width, units = weights[0].shape
    total = 2 * m * len(plans)
    cuts = tiles_of(units, 512)

    def body(spot0_ref, spot1_ref, *refs):
        groups = dict(zip(used, refs))
        w_hbm = refs[len(used) : len(used) + 2]
        g_ref, u_ref, x_ref, buffers, sems = refs[-5:]

        def use(i, w_ref):
            (g_ref, u_ref)[i % 2][:, cuts[i // 2]] = jnp.dot(
                x_ref[...], w_ref[...], preferred_element_type=F32
            ).astype(BF16)

        pieces = [w.at[:, c] for c in cuts for w in w_hbm]
        run = streamed(pieces, buffers, sems, use)
        for r, plan in enumerate(plans):
            for f in range(2):
                options = [
                    jnp.zeros((m, width), BF16) if c is None else groups[c[0]][c[1] : c[1] + m, :]
                    for c in plan[f]
                ]
                at = (2 * r + f) * m
                x_ref[at : at + m] = pick(options, (spot0_ref, spot1_ref)[f][0])
        for i in range(len(pieces)):
            run(i)

    args = (*spot, *(rows[j] for j in used), *weights, *ties)
    slots = min(8, 2 * len(cuts))
    return call(
        body,
        "project",
        [array(total, units)] * 2,
        args,
        [SCALAR] * 2 + [WHOLE] * len(used) + [FAR] * 2 + [WHOLE] * len(ties),
        [
            pltpu.VMEM((total, width), BF16),
            pltpu.VMEM((slots, width, units // len(cuts)), BF16),
            pltpu.SemaphoreType.DMA((slots,)),
        ],
        grant=48,
    )


def combine(m, units, f, first, came, partial, act, summing, sending, fresh, spot, ties, relay=()):
    args, use = [], {}

    def take(key, value):
        if value is not None:
            use[key] = len(args)
            args.append(value)

    take("spot", spot if act is not None and came is not None else None)
    take("came", came)
    if summing:
        take("g", partial[0])
        take("u", partial[1])
        base = partial[2] + f * m
    take("act", act)
    for k, value in enumerate(relay):
        take(k, value)
    taken = len(args)
    args += ties
    sums = 2 * m if summing and sending else 0
    hidden = act is not None or (came is not None and came.shape[0] % (2 * m) == m)
    rows = sums + (m if hidden else 0)
    shapes = [array(rows, units)] if rows else []
    if fresh:
        shapes.append(array(m, units))
    for value in relay:
        shapes.append(array(*value.shape))

    def body(*refs):
        ins, outs = refs[:taken], refs[len(args) :]
        ref = {key: ins[at] for key, at in use.items()}
        for k in range(len(relay)):
            outs[len(shapes) - len(relay) + k][...] = ref[k][...]

        def step(cols):
            if summing:
                total = []
                for k, key in enumerate(("g", "u")):
                    value = ref[key][base : base + m, cols].astype(F32)
                    if not first:
                        value = value + ref["came"][k * m : (k + 1) * m, cols].astype(F32)
                    total.append(value)
                    if sending:
                        outs[0][k * m : (k + 1) * m, cols] = value.astype(BF16)
                if fresh:
                    g, u = total
                    outs[1 if rows else 0][:, cols] = (g / (1.0 + jnp.exp(-g)) * u).astype(BF16)
            if hidden:
                if "came" in ref and came.shape[0] % (2 * m) == m:
                    h = ref["came"][came.shape[0] - m :, cols]
                    if "act" in ref:
                        h = jnp.where(ref["spot"][0] == 0, ref["act"][:, cols], h)
                else:
                    h = ref["act"][:, cols]
                outs[0][sums:, cols] = h

        wide = 512 if units % 512 == 0 else units

        def loop(i, carry):
            step(pl.ds(pl.multiple_of(i * wide, wide), wide))
            return carry

        lax.fori_loop(0, units // wide, loop, 0)

    out = list(call(body, "combine", shapes, args))
    relayed = [out.pop() for _ in relay][::-1]
    activated = out.pop() if fresh else None
    return (out[0] if rows else None), activated, relayed


def lower(m, pairs, wd, tie):
    units, columns = wd.shape
    total = 2 * m * len(pairs)
    cuts = tiles_of(units, 512)
    flat = [message for pair in pairs for message in pair]

    def body(*refs):
        messages, w_hbm = refs[: len(flat)], refs[len(flat)]
        out_ref, sum_ref, buffers, sems = refs[-4:]

        def use(i, w_ref):
            h = jnp.concatenate([r[r.shape[0] - m :, cuts[i]] for r in messages])
            part = jnp.dot(h, w_ref[...], preferred_element_type=F32)
            if i:
                part = part + sum_ref[...]
            if i == len(cuts) - 1:
                out_ref[...] = part.astype(BF16)
            else:
                sum_ref[...] = part

        run = streamed([w_hbm.at[c, :] for c in cuts], buffers, sems, use)
        for i in range(len(cuts)):
            run(i)

    slots = min(6, len(cuts))
    return call(
        body,
        "lower",
        [array(total, columns)],
        (*flat, wd, *tie),
        [WHOLE] * len(flat) + [FAR] + [WHOLE] * len(tie),
        [
            pltpu.VMEM((total, columns), F32),
            pltpu.VMEM((slots, units // len(cuts), columns), BF16),
            pltpu.SemaphoreType.DMA((slots,)),
        ],
        grant=48,
    )[0]


def mix(m, experts, half, places, gates, spans, parts):
    n, width = gates.shape[0], parts[0].shape[1]

    def body(place_ref, gate_ref, *refs):
        total = jnp.zeros((n, width), F32)
        for k in range(2):
            y = jnp.zeros((n, width), F32)
            for (j, start, stop, i), part_ref in zip(spans, refs):
                rows = (stop - start) * m
                for f in range(2):
                    rank = lax.broadcasted_iota(I32, (rows, n), 0) + (i * m + f * half)
                    chosen = one_hot(rank * experts + j == place_ref[k : k + 1, :])
                    y += lax.dot_general(
                        chosen,
                        part_ref[f * rows : (f + 1) * rows, :],
                        (((0,), (0,)), ((), ())),
                        preferred_element_type=F32,
                    )
            total += gate_ref[:, k : k + 1] * y
        refs[-1][...] = total.astype(BF16)

    specs = [WHOLE] * (2 + len(parts))
    return call(body, "mix", [array(n, width)], (places, gates, *parts), specs)[0]


def local(tokens, route_ids, gates, w_gate, w_up, w_down):
    experts = lax.axis_size("expert")
    depth = lax.axis_size("dp")
    tensors = lax.axis_size("tensor")
    z = lax.axis_index("dp")
    e = lax.axis_index("expert")
    n, width = tokens.shape
    units = w_gate.shape[2]
    capacity = max(3 * n // 8, 2 * n // experts)
    capacity = (capacity + 15) // 16 * 16
    half = capacity // 2
    m = CHUNK if half % CHUNK == 0 else 16
    per = half // m
    order = chunk_order(experts, per)
    chunks = len(order)
    last = depth - 1

    even = e % 2 == 0
    spot = [jnp.where(even, z, last - z), jnp.where(even, last - z, z)]
    spot = [a.astype(I32).reshape(1) for a in spot]
    climb = [(a * experts + b, (a + 1) * experts + b) for a in range(last) for b in range(experts)]
    flows = [[(a, c) if a % experts % 2 == f else (c, a) for a, c in climb] for f in range(2)]

    weights = (w_gate[0], w_up[0])
    wd = w_down[0]
    places, picked, marks, opening = begin(
        m, experts, capacity, e.astype(I32).reshape(1), spot, route_ids.T, tokens, *weights
    )
    rows = [picked[0]]

    def sources(s):
        found = [[None] * depth for _ in range(2)]
        for f in range(2):
            for a in range(depth):
                if 0 <= s - a < chunks:
                    j, i = order[s - a]
                    found[f][a] = (j, f * half + i * m)
        return found

    def across(part):
        if tensors == 2:
            other = lax.ppermute(part, "tensor", [(0, 1), (1, 0)])
            return (part.astype(F32) + other.astype(F32)).astype(BF16)
        return lax.psum(part, "tensor")

    sums_end = chunks + last
    ticks = chunks + 2 * last + 1
    ends = chunks + last
    partial = {0: (*opening, 0)}
    got = [None, None]
    act = [None, None]
    held = [{}, {}]
    outs = {}
    ties = []
    spans = []
    for index, (j, i) in enumerate(order):
        if spans and spans[-1][0] == j:
            spans[-1][2] = index + 1
        else:
            spans.append([j, index, index + 1, i])
    def rounds_of(start, stop):
        return range(start, stop + last)

    def own_copy(start, stop):
        return lax.optimization_barrier([outs[q] for q in rounds_of(start, stop)])

    def finished(start, stop):
        outs = dict(zip(rounds_of(start, stop), own_copy(start, stop)))
        return [
            jnp.concatenate(
                [
                    pick(
                        [outs[c + a][f * m : (f + 1) * m] for a in range(depth)],
                        marks[8 * (1 - f) : 8 * (1 - f) + 1, :1],
                    )
                    for c in range(start, stop)
                ]
            )
            for f in range(2)
        ]

    parts, sent = [None] * len(spans), set()

    def ready_spans():
        fresh = []
        for index, (j, start, stop, i) in enumerate(spans):
            if index not in sent and all(q in outs for q in rounds_of(start, stop)):
                sent.add(index)
                fresh.append((index, lax.optimization_barrier(jnp.concatenate(finished(start, stop)))))
        return fresh

    def forward(index, part):
        j = spans[index][0]
        if j:
            part = lax.ppermute(part, "expert", [(a, a ^ j) for a in range(experts)])
        parts[index] = part

    def deliver():
        for index, part in ready_spans():
            forward(index, part)

    def settle(ready, result):
        for k, q in enumerate(ready):
            outs[q] = result[2 * m * k : 2 * m * (k + 1)]

    lowered = None
    for s in range(ticks):
        summing = s < sums_end
        for f in range(2):
            o = 1 - f
            first = last + 1 if f == 0 else last
            carries = first <= s < first + chunks + last
            if not (summing or carries):
                continue
            relay, moving = (), ()
            if f == 1:
                moving = ready_spans() if s < ticks - 2 else ()
                relay = list(picked[1:]) if s == 0 else [part for _, part in moving]
                relay += [lowered[1]] if lowered else []
            message, act[f], relayed = combine(
                m,
                units,
                f,
                s == 0,
                got[f] if s else None,
                partial.get(s),
                act[o] if carries else None,
                summing,
                s < sums_end - 1,
                summing and s >= last,
                spot[f],
                ties,
                relay,
            )
            ties = []
            if s < sums_end - 1 or (carries and s < first + chunks + last - 1):
                got[f] = lax.ppermute(message, ("dp", "expert"), flows[f])
            if s == 0:
                for j, value in enumerate(relayed, 1):
                    rows.append(lax.ppermute(value, "expert", [(a, a ^ j) for a in range(experts)]))
            elif relayed:
                for (index, _), part in zip(moving, relayed):
                    forward(index, part)
                    ties.append(parts[index])
                if lowered:
                    settle(lowered[0], across(relayed[-1]))
                    ties.append(outs[lowered[0][0]])
                    lowered = None
            if s == 1 and f == 1:
                ties += rows[2:]
            if carries:
                held[o][s - first] = message
            if f == (0 if s else 1) and s + 1 < sums_end and s + 1 not in partial:
                rounds = [r for r in (s + 1, s + 2) if r < sums_end]
                wait = [message]
                g, u = project(m, spot, rows, [sources(r) for r in rounds], weights, wait)
                for k, r in enumerate(rounds):
                    partial[r] = (g, u, 2 * m * k)
                ties.append(g)
            ready = [q for q in range(ends) if q in held[0] and q in held[1] and q not in outs]
            if len(ready) == 2 or (ready and ready[0] == ends - 1):
                pairs = [(held[0][q], held[1][q]) for q in ready]
                if ready[0] == ends - 1:
                    deliver()
                arrived = [p for p in parts if p is not None] if ready[0] == ends - 1 else []
                result = lower(m, pairs, wd, [message] + arrived)
                if f == 0 and s < ticks - 1:
                    lowered = (ready, result)
                else:
                    ties.append(result)
                    settle(ready, across(result))

    deliver()
    return mix(m, experts, half, places, gates, spans, parts)


def solution(mesh):
    return jax.shard_map(
        local,
        mesh=mesh,
        in_specs=(
            P("expert", "dp"),
            P("expert", None),
            P("expert", None),
            P("expert", "dp", "tensor"),
            P("expert", "dp", "tensor"),
            P("expert", "tensor", "dp"),
        ),
        out_specs=P("expert", "dp"),
        check_vma=False,
    )
```

```python
import jax
import jax.numpy as jnp
import numpy as np
from jax import lax
from jax.experimental import pallas as pl
from jax.experimental.pallas import tpu as pltpu
from jax.sharding import PartitionSpec as P

F32, BF16, I32 = jnp.float32, jnp.bfloat16, jnp.int32
CHUNK = 32
WHOLE = pl.BlockSpec(memory_space=pltpu.VMEM)
SCALAR = pl.BlockSpec(memory_space=pltpu.SMEM)
FAR = pl.BlockSpec(memory_space=pltpu.HBM)
LIGHT = pl.CostEstimate(flops=0, bytes_accessed=0, transcendentals=0)


def chunk_order(experts, per):
    head = max(1, per // 2)
    order = [(0, i) for i in range(head)]
    order += [(j, i) for j in range(1, experts) for i in range(per)]
    return order + [(0, i) for i in range(head, per)]


def pick(options, index):
    out = options[-1]
    for k in range(len(options) - 2, -1, -1):
        out = jnp.where(index == k, options[k], out)
    return out


def array(*shape, dtype=BF16):
    return jax.ShapeDtypeStruct(shape, dtype)


def call(body, name, shapes, args, specs=None, scratch=(), grant=16):
    if specs is None:
        specs = [SCALAR if a.dtype == I32 else WHOLE for a in args]
    return pl.pallas_call(
        body,
        name=name,
        out_shape=shapes,
        in_specs=specs,
        out_specs=[WHOLE] * len(shapes),
        scratch_shapes=scratch,
        cost_estimate=LIGHT,
        compiler_params=pltpu.CompilerParams(vmem_limit_bytes=grant * 2**20),
    )(*args)


def tiles_of(columns, wide):
    wide = wide if columns % wide == 0 else columns
    return [pl.ds(at, wide) for at in range(0, columns, wide)]


def one_hot(mask):
    return jnp.where(mask, 1.0, 0.0).astype(BF16)


def streamed(pieces, buffers, sems, use):
    slots = buffers.shape[0]

    def load(i):
        return pltpu.make_async_copy(pieces[i], buffers.at[i % slots], sems.at[i % slots])

    for i in range(min(slots, len(pieces))):
        load(i).start()

    def run(i):
        load(i).wait()
        use(i, buffers.at[i % slots])
        if i + slots < len(pieces):
            load(i + slots).start()

    return run


def begin(m, experts, capacity, e, spot, ids, tokens, wg, wu):
    n, width = tokens.shape
    units = wg.shape[1]
    half = capacity // 2
    cuts = tiles_of(units, 512)
    names = (experts + 15) // 16 * 16

    def body(e_ref, spot0_ref, spot1_ref, ids_hbm, tok_hbm, wg_hbm, wu_hbm, place_ref, *rest):
        rows = rest[:experts]
        mark_ref, g_ref, u_ref, x_ref, ids_ref, tok_ref, buffers, sems, small = rest[experts:]
        ids_copy = pltpu.make_async_copy(ids_hbm, ids_ref, small.at[0])
        tok_copy = pltpu.make_async_copy(tok_hbm, tok_ref, small.at[1])
        ids_copy.start()
        tok_copy.start()

        def use(i, w_ref):
            (g_ref, u_ref)[i % 2][:, cuts[i // 2]] = jnp.dot(
                x_ref[...], w_ref[...], preferred_element_type=F32
            ).astype(BF16)

        pieces = [w.at[:, c] for c in cuts for w in (wg_hbm, wu_hbm)]
        run = streamed(pieces, buffers, sems, use)
        ids_copy.wait()
        index = lax.broadcasted_iota(I32, (names, n), 0)
        ids = [ids_ref[k : k + 1, :] ^ e_ref[0] for k in range(2)]
        mark_ref[:8] = jnp.full((8, 128), spot0_ref[0], I32)
        mark_ref[8:] = jnp.full((8, 128), spot1_ref[0], I32)
        hits = [index == ids[k] for k in range(2)]
        earlier = lax.broadcasted_iota(I32, (n, n), 0) < lax.broadcasted_iota(I32, (n, n), 1)
        before = jnp.dot(one_hot(hits[0] | hits[1]), one_hot(earlier), preferred_element_type=F32)
        places = []
        for k in range(2):
            rank = jnp.sum(jnp.where(hits[k], before, 0.0), axis=0, keepdims=True)
            places.append(rank.astype(I32) * experts + ids[k])
            place_ref[k : k + 1, :] = places[k]
        lines = lax.broadcasted_iota(I32, (capacity, n), 0) * experts
        tok_copy.wait()
        for j in range(experts):
            mine = lines + j
            chosen = one_hot((mine == places[0]) | (mine == places[1]))
            picked = jnp.dot(chosen, tok_ref[...], preferred_element_type=F32).astype(BF16)
            rows[j][...] = picked
            if j == 0:
                x_ref[:m] = picked[:m]
                x_ref[m:] = picked[half : half + m]
        for i in range(len(pieces)):
            run(i)

    shapes = [array(2, n, dtype=I32)] + [array(capacity, width)] * experts
    shapes += [array(16, 128, dtype=I32)] + [array(2 * m, units)] * 2
    slots = 2 * len(cuts)
    out = call(
        body,
        "begin",
        shapes,
        (e, *spot, ids, tokens, wg, wu),
        [SCALAR] * 3 + [FAR] * 4,
        [
            pltpu.VMEM((2 * m, width), BF16),
            pltpu.VMEM((2, n), I32),
            pltpu.VMEM((n, width), BF16),
            pltpu.VMEM((slots, width, units // len(cuts)), BF16),
            pltpu.SemaphoreType.DMA((slots,)),
            pltpu.SemaphoreType.DMA((2,)),
        ],
        grant=48,
    )
    return out[0], out[1 : 1 + experts], out[1 + experts], out[2 + experts :]


def project(m, spot, rows, plans, weights, ties):
    used = sorted({c[0] for plan in plans for per_flow in plan for c in per_flow if c})
    width, units = weights[0].shape
    total = 2 * m * len(plans)
    cuts = tiles_of(units, 512)

    def body(spot0_ref, spot1_ref, *refs):
        groups = dict(zip(used, refs))
        w_hbm = refs[len(used) : len(used) + 2]
        g_ref, u_ref, x_ref, buffers, sems = refs[-5:]

        def use(i, w_ref):
            (g_ref, u_ref)[i % 2][:, cuts[i // 2]] = jnp.dot(
                x_ref[...], w_ref[...], preferred_element_type=F32
            ).astype(BF16)

        pieces = [w.at[:, c] for c in cuts for w in w_hbm]
        run = streamed(pieces, buffers, sems, use)
        for r, plan in enumerate(plans):
            for f in range(2):
                options = [
                    jnp.zeros((m, width), BF16) if c is None else groups[c[0]][c[1] : c[1] + m, :]
                    for c in plan[f]
                ]
                at = (2 * r + f) * m
                x_ref[at : at + m] = pick(options, (spot0_ref, spot1_ref)[f][0])
        for i in range(len(pieces)):
            run(i)

    args = (*spot, *(rows[j] for j in used), *weights, *ties)
    slots = min(8, 2 * len(cuts))
    return call(
        body,
        "project",
        [array(total, units)] * 2,
        args,
        [SCALAR] * 2 + [WHOLE] * len(used) + [FAR] * 2 + [WHOLE] * len(ties),
        [
            pltpu.VMEM((total, width), BF16),
            pltpu.VMEM((slots, width, units // len(cuts)), BF16),
            pltpu.SemaphoreType.DMA((slots,)),
        ],
        grant=48,
    )


def combine(m, units, f, first, came, partial, act, summing, sending, fresh, spot, ties, relay=()):
    args, use = [], {}

    def take(key, value):
        if value is not None:
            use[key] = len(args)
            args.append(value)

    take("spot", spot if act is not None and came is not None else None)
    take("came", came)
    if summing:
        take("g", partial[0])
        take("u", partial[1])
        base = partial[2] + f * m
    take("act", act)
    for k, value in enumerate(relay):
        take(k, value)
    taken = len(args)
    args += ties
    sums = 2 * m if summing and sending else 0
    hidden = act is not None or (came is not None and came.shape[0] % (2 * m) == m)
    rows = sums + (m if hidden else 0)
    shapes = [array(rows, units)] if rows else []
    if fresh:
        shapes.append(array(m, units))
    for value in relay:
        shapes.append(array(*value.shape))

    def body(*refs):
        ins, outs = refs[:taken], refs[len(args) :]
        ref = {key: ins[at] for key, at in use.items()}
        for k in range(len(relay)):
            outs[len(shapes) - len(relay) + k][...] = ref[k][...]

        def step(cols):
            if summing:
                total = []
                for k, key in enumerate(("g", "u")):
                    value = ref[key][base : base + m, cols].astype(F32)
                    if not first:
                        value = value + ref["came"][k * m : (k + 1) * m, cols].astype(F32)
                    total.append(value)
                    if sending:
                        outs[0][k * m : (k + 1) * m, cols] = value.astype(BF16)
                if fresh:
                    g, u = total
                    outs[1 if rows else 0][:, cols] = (g / (1.0 + jnp.exp(-g)) * u).astype(BF16)
            if hidden:
                if "came" in ref and came.shape[0] % (2 * m) == m:
                    h = ref["came"][came.shape[0] - m :, cols]
                    if "act" in ref:
                        h = jnp.where(ref["spot"][0] == 0, ref["act"][:, cols], h)
                else:
                    h = ref["act"][:, cols]
                outs[0][sums:, cols] = h

        wide = 512 if units % 512 == 0 else units

        def loop(i, carry):
            step(pl.ds(pl.multiple_of(i * wide, wide), wide))
            return carry

        lax.fori_loop(0, units // wide, loop, 0)

    out = list(call(body, "combine", shapes, args))
    relayed = [out.pop() for _ in relay][::-1]
    activated = out.pop() if fresh else None
    return (out[0] if rows else None), activated, relayed


def lower(m, pairs, wd, tie):
    units, columns = wd.shape
    total = 2 * m * len(pairs)
    cuts = tiles_of(units, 512)
    flat = [message for pair in pairs for message in pair]

    def body(*refs):
        messages, w_hbm = refs[: len(flat)], refs[len(flat)]
        out_ref, sum_ref, buffers, sems = refs[-4:]

        def use(i, w_ref):
            h = jnp.concatenate([r[r.shape[0] - m :, cuts[i]] for r in messages])
            part = jnp.dot(h, w_ref[...], preferred_element_type=F32)
            if i:
                part = part + sum_ref[...]
            if i == len(cuts) - 1:
                out_ref[...] = part.astype(BF16)
            else:
                sum_ref[...] = part

        run = streamed([w_hbm.at[c, :] for c in cuts], buffers, sems, use)
        for i in range(len(cuts)):
            run(i)

    slots = min(6, len(cuts))
    return call(
        body,
        "lower",
        [array(total, columns)],
        (*flat, wd, *tie),
        [WHOLE] * len(flat) + [FAR] + [WHOLE] * len(tie),
        [
            pltpu.VMEM((total, columns), F32),
            pltpu.VMEM((slots, units // len(cuts), columns), BF16),
            pltpu.SemaphoreType.DMA((slots,)),
        ],
        grant=48,
    )[0]


def mix(m, experts, half, places, gates, spans, parts):
    n, width = gates.shape[0], parts[0].shape[1]

    def body(place_ref, gate_ref, *refs):
        total = jnp.zeros((n, width), F32)
        for k in range(2):
            y = jnp.zeros((n, width), F32)
            for (j, start, stop, i), part_ref in zip(spans, refs):
                rows = (stop - start) * m
                for f in range(2):
                    rank = lax.broadcasted_iota(I32, (rows, n), 0) + (i * m + f * half)
                    chosen = one_hot(rank * experts + j == place_ref[k : k + 1, :])
                    y += lax.dot_general(
                        chosen,
                        part_ref[f * rows : (f + 1) * rows, :],
                        (((0,), (0,)), ((), ())),
                        preferred_element_type=F32,
                    )
            total += gate_ref[:, k : k + 1] * y
        refs[-1][...] = total.astype(BF16)

    specs = [WHOLE] * (2 + len(parts))
    return call(body, "mix", [array(n, width)], (places, gates, *parts), specs)[0]


def local(tokens, route_ids, gates, w_gate, w_up, w_down):
    experts = lax.axis_size("expert")
    depth = lax.axis_size("dp")
    tensors = lax.axis_size("tensor")
    z = lax.axis_index("dp")
    e = lax.axis_index("expert")
    n, width = tokens.shape
    units = w_gate.shape[2]
    capacity = max(3 * n // 8, 2 * n // experts)
    capacity = (capacity + 15) // 16 * 16
    half = capacity // 2
    m = CHUNK if half % CHUNK == 0 else 16
    per = half // m
    order = chunk_order(experts, per)
    chunks = len(order)
    last = depth - 1

    even = e % 2 == 0
    spot = [jnp.where(even, z, last - z), jnp.where(even, last - z, z)]
    spot = [a.astype(I32).reshape(1) for a in spot]
    climb = [(a * experts + b, (a + 1) * experts + b) for a in range(last) for b in range(experts)]
    flows = [[(a, c) if a % experts % 2 == f else (c, a) for a, c in climb] for f in range(2)]

    weights = (w_gate[0], w_up[0])
    wd = w_down[0]
    places, picked, marks, opening = begin(
        m, experts, capacity, e.astype(I32).reshape(1), spot, route_ids.T, tokens, *weights
    )
    rows = [picked[0]]

    def sources(s):
        found = [[None] * depth for _ in range(2)]
        for f in range(2):
            for a in range(depth):
                if 0 <= s - a < chunks:
                    j, i = order[s - a]
                    found[f][a] = (j, f * half + i * m)
        return found

    def across(part):
        if tensors == 2:
            other = lax.ppermute(part, "tensor", [(0, 1), (1, 0)])
            return (part.astype(F32) + other.astype(F32)).astype(BF16)
        return lax.psum(part, "tensor")

    sums_end = chunks + last
    ticks = chunks + 2 * last + 1
    ends = chunks + last
    partial = {0: (*opening, 0)}
    got = [None, None]
    act = [None, None]
    held = [{}, {}]
    outs = {}
    ties = []
    spans = []
    for index, (j, i) in enumerate(order):
        if spans and spans[-1][0] == j:
            spans[-1][2] = index + 1
        else:
            spans.append([j, index, index + 1, i])
    def rounds_of(start, stop):
        return range(start, stop + last)

    def own_copy(start, stop):
        return lax.optimization_barrier([outs[q] for q in rounds_of(start, stop)])

    def finished(start, stop):
        outs = dict(zip(rounds_of(start, stop), own_copy(start, stop)))
        return [
            jnp.concatenate(
                [
                    pick(
                        [outs[c + a][f * m : (f + 1) * m] for a in range(depth)],
                        marks[8 * (1 - f) : 8 * (1 - f) + 1, :1],
                    )
                    for c in range(start, stop)
                ]
            )
            for f in range(2)
        ]

    parts = []

    def deliver():
        for j, start, stop, i in spans[len(parts) :]:
            if all(q in outs for q in rounds_of(start, stop)):
                part = lax.optimization_barrier(jnp.concatenate(finished(start, stop)))
                if j:
                    part = lax.ppermute(part, "expert", [(a, a ^ j) for a in range(experts)])
                parts.append(part)

    for s in range(ticks):
        summing = s < sums_end
        for f in range(2):
            o = 1 - f
            first = last + 1 if f == 0 else last
            carries = first <= s < first + chunks + last
            if not (summing or carries):
                continue
            message, act[f], relayed = combine(
                m,
                units,
                f,
                s == 0,
                got[f] if s else None,
                partial.get(s),
                act[o] if carries else None,
                summing,
                s < sums_end - 1,
                summing and s >= last,
                spot[f],
                ties,
                picked[1:] if s == 0 and f == 1 else (),
            )
            ties = []
            if s < sums_end - 1 or (carries and s < first + chunks + last - 1):
                got[f] = lax.ppermute(message, ("dp", "expert"), flows[f])
            for j, value in enumerate(relayed, 1):
                rows.append(lax.ppermute(value, "expert", [(a, a ^ j) for a in range(experts)]))
            if s == 1 and f == 1:
                ties += rows[2:]
            if carries:
                held[o][s - first] = message
            if f == (0 if s else 1) and s + 1 < sums_end and s + 1 not in partial:
                rounds = [r for r in (s + 1, s + 2) if r < sums_end]
                wait = [message]
                g, u = project(m, spot, rows, [sources(r) for r in rounds], weights, wait)
                for k, r in enumerate(rounds):
                    partial[r] = (g, u, 2 * m * k)
                ties.append(g)
            ready = [q for q in range(ends) if q in held[0] and q in held[1] and q not in outs]
            if len(ready) == 2 or (ready and ready[0] == ends - 1):
                pairs = [(held[0][q], held[1][q]) for q in ready]
                if ready[0] == ends - 1:
                    deliver()
                result = lower(m, pairs, wd, [message] + (parts if ready[0] == ends - 1 else []))
                ties.append(result)
                result = across(result)
                for k, q in enumerate(ready):
                    outs[q] = result[2 * m * k : 2 * m * (k + 1)]

    deliver()
    return mix(m, experts, half, places, gates, spans, parts)


def solution(mesh):
    return jax.shard_map(
        local,
        mesh=mesh,
        in_specs=(
            P("expert", "dp"),
            P("expert", None),
            P("expert", None),
            P("expert", "dp", "tensor"),
            P("expert", "dp", "tensor"),
            P("expert", "tensor", "dp"),
        ),
        out_specs=P("expert", "dp"),
        check_vma=False,
    )
```
